32 devices in a mesh: dom: 8 (over y, x, core), band: 4 (over z).
Axes of the slice: x: 2, y: 2, z: 4, core: 2. Of those that a mesh axis runs over, the one named last changes fastest.
Arguments:
- states: bfloat16 [256, 98304], P('band', 'dom'), may hold values from -640 to 640
- cell_kinetic: bfloat16 [512, 512], replicated, may hold values from -0.3 to 0.3, as said below
- cell_scale: float32 [256], P('dom'), may hold values from 0.5 to 2
- cell_potential: float32 [256, 512], P('dom'), may hold values from -0.3 to 0.3
- connectivity: int32 [256, 512], P('dom'), may hold values from 0 to 12287, as said below
- shared_nodes: int32 [8, 2, 1024], P('dom'), may hold values from 0 to 12287, as said below
- cell_counts: int32 [8], P('dom'), may hold values from 4 to 32, as said below
Outputs:
- rotated: bfloat16 [256, 98304], P('band', 'dom')
The draws below stay inside these ranges and needn't reach their ends.
Inputs may be any that keep to these rules, and one draw needn't show every extreme that they name: cell_kinetic is symmetric. `connectivity`: row c of a domain (local cell number c) names each of the 512 nodes c * 3 * 128 to c * 3 * 128 + 511, counted round modulo 12288, exactly once. `shared_nodes`: the two rows of a domain name 2048 distinct nodes; position p of domain d's row 1 and of domain d+1's row 0 are the same physical node. `cell_counts`: in every draw some domain has all 32 cells live.
All inputs are finite; a program needn't handle non-finite values.
Results may differ from the reference program's by a relative error of at most 0.008.
Values may be sent and summed in bfloat16 or wider, within the bound.
A program may use at most 128 MiB of HBM per device.

```python
import math
import jax
import jax.numpy as jnp
from jax import lax

NP = 512
S = 256
CELLS_DEV = 32
CHEB = 4
NS_ITERS = 5
NODES = 12288
SHARED = 1024
CELLS = 256
NODES_ALL = 98304
N_DOM = 8


def draw_states(key, part):
    base_key, state_key = jax.random.split(key, 2)
    pair_key = jax.random.fold_in(key, 31)
    node_scale = 1.0 + 0.75 * jnp.arange(NODES_ALL, dtype=jnp.float32) / NODES_ALL
    state_scale = jnp.exp(jax.random.uniform(state_key, (S,), jnp.float32, 0.0, math.log(10.0)))
    offset = jax.random.randint(pair_key, (), 0, N_DOM, dtype=jnp.int32)
    partner = (jnp.arange(S, dtype=jnp.int32) + offset) % N_DOM
    node_domain = jnp.arange(NODES_ALL, dtype=jnp.int32) // NODES
    spike = jnp.where(node_domain[None, :] == partner[:, None], 6.0, 1.0).astype(jnp.float32)
    values = jnp.clip(jax.random.normal(base_key, (S, NODES_ALL), jnp.float32), -6.0, 6.0)
    return (values * spike * state_scale[:, None] * node_scale[None]).astype(jnp.bfloat16)


def draw_cell_kinetic(key, part):
    raw = jnp.clip(jax.random.normal(key, (NP, NP), jnp.float32), -4.0, 4.0)
    return (0.15 * jnp.eye(NP, dtype=jnp.float32) + (raw + raw.T) * (0.1 / math.sqrt(NP))).astype(jnp.bfloat16)


def draw_connectivity(key, part):
    order_key = jax.random.fold_in(key, 11)
    local_cell = jnp.arange(CELLS, dtype=jnp.int32) % CELLS_DEV
    window = jax.random.permutation(order_key, jnp.broadcast_to(jnp.arange(NP, dtype=jnp.int32), (CELLS, NP)), axis=1, independent=True)
    return (local_cell[:, None] * (NP * 3 // 4) + window) % NODES


def draw_shared_nodes(key, part):
    shuffled = jax.random.permutation(key, jnp.broadcast_to(jnp.arange(NODES, dtype=jnp.int32), (N_DOM, NODES)), axis=1, independent=True)
    return jnp.stack([shuffled[:, :SHARED], shuffled[:, SHARED:2 * SHARED]], axis=1)


def draw_cell_counts(key, part):
    first_key = jax.random.fold_in(key, 21)
    second_key = jax.random.fold_in(key, 22)
    full_key = jax.random.fold_in(key, 23)
    lowest = max(1, CELLS_DEV // 8)
    first = jax.random.randint(first_key, (N_DOM,), lowest, CELLS_DEV + 1, dtype=jnp.int32)
    second = jax.random.randint(second_key, (N_DOM,), lowest, CELLS_DEV + 1, dtype=jnp.int32)
    counts = jnp.minimum(first, second)
    fullest = jax.random.randint(full_key, (), 0, N_DOM, dtype=jnp.int32)
    return counts.at[fullest].set(CELLS_DEV)


def level_of(key, shape, shards, low, largest):
    loudness, own = 1.0, jax.random.fold_in(key, 6)
    for dim, blocks in shards:
        draws = jnp.exp(jax.random.uniform(jax.random.fold_in(own, dim), (blocks,), jnp.float32, low / len(shards), largest / len(shards)))
        loudness = loudness * jnp.repeat(draws, shape[dim] // blocks).reshape([-1 if axis == dim else 1 for axis in range(len(shape))])
    return loudness


def setup_inputs(seed: int = 0) -> dict:
    splits = jax.random.split(jax.random.key(seed), 8)
    states = draw_states(jax.random.fold_in(splits[7], 71), 0)
    cell_kinetic = draw_cell_kinetic(jax.random.fold_in(splits[7], 71), 0)
    cell_scale = jnp.clip(jnp.exp(math.log(2.0) - 1.3862944 * jax.random.uniform(splits[2], (CELLS,), jnp.float32) ** level_of(splits[2], (CELLS,), ((0, 8),), -0.2, 0.2)), 0.5, 2.0)
    cell_potential = jnp.clip(jax.random.uniform(splits[3], (CELLS, NP), jnp.float32, -0.3, 0.3) * level_of(splits[3], (CELLS, NP), ((0, 8),), -0.4, 0.0), -0.3, 0.3)
    connectivity = draw_connectivity(jax.random.fold_in(splits[7], 71), 0)
    shared_nodes = draw_shared_nodes(jax.random.fold_in(splits[7], 71), 0)
    cell_counts = draw_cell_counts(jax.random.fold_in(splits[7], 71), 0)
    return {"states": states, "cell_kinetic": cell_kinetic, "cell_scale": cell_scale, "cell_potential": cell_potential, "connectivity": connectivity, "shared_nodes": shared_nodes, "cell_counts": cell_counts}


def pick_columns(field, positions):
    return field[:, positions]

def add_faces(field, left_row, right_row, left_add, right_add):
    return field.at[:, left_row].add(left_add).at[:, right_row].add(right_add)

def count_uses(left_row, right_row, left_flag, right_flag):
    return jnp.ones((NODES,), jnp.float32).at[left_row].add(left_flag).at[right_row].add(right_flag)

def reference(states, cell_kinetic, cell_scale, cell_potential, connectivity, shared_nodes, cell_counts):
    kinetic = cell_kinetic.astype(jnp.float32)
    scales = cell_scale.reshape(N_DOM, CELLS_DEV)
    potential = cell_potential.reshape(N_DOM, CELLS_DEV, NP)
    connect = connectivity.reshape(N_DOM, CELLS_DEV, NP)
    left_face = shared_nodes[:, 0]
    right_face = shared_nodes[:, 1]

    def local_domain(packed):
        vector, scale_row, potential_rows, conn_rows, live_count = packed
        gathered = vector[:, conn_rows].astype(jnp.float32)
        product = jnp.einsum('scj,ij->sci', gathered, kinetic)
        alive_mask = (jnp.arange(CELLS_DEV) < live_count).astype(jnp.float32)
        cell_terms = (product * scale_row[None, :, None] + potential_rows[None] * gathered) * alive_mask[None, :, None]
        return jnp.zeros((S, NODES), jnp.float32).at[:, conn_rows].add(cell_terms)

    def apply_field(fields):
        local_sum = lax.map(local_domain, (fields, scales, potential, connect, cell_counts))
        right_values = jax.vmap(pick_columns)(local_sum, right_face)
        left_values = jax.vmap(pick_columns)(local_sum, left_face)
        zero_face = jnp.zeros_like(right_values[:1])
        from_left = jnp.concatenate([zero_face, right_values[:-1]], axis=0)
        from_right = jnp.concatenate([left_values[1:], zero_face], axis=0)
        return jax.vmap(add_faces)(local_sum, left_face, right_face, from_left, from_right)
    fields = states.reshape(S, N_DOM, NODES).transpose(1, 0, 2)
    previous = fields
    current = apply_field(fields).astype(jnp.bfloat16)
    for repeat in range(CHEB - 1):
        following = (2.0 * apply_field(current) - previous.astype(jnp.float32)).astype(jnp.bfloat16)
        previous = current
        current = following
    has_left = (jnp.arange(N_DOM) > 0).astype(jnp.float32)
    has_right = (jnp.arange(N_DOM) < N_DOM - 1).astype(jnp.float32)
    multiplicity = jax.vmap(count_uses)(left_face, right_face, has_left, has_right)
    node_weight = (1.0 / multiplicity).astype(jnp.bfloat16)

    def add_domain(carry, packed):
        field, weight_row = packed
        weighted = field * weight_row[None]
        return (carry + jnp.dot(weighted, field.T, preferred_element_type=jnp.float32), None)
    gram_matrix, unused = lax.scan(add_domain, jnp.zeros((S, S), jnp.float32), (current, node_weight))
    identity = jnp.eye(S, dtype=jnp.float32)
    frobenius = jnp.sqrt(jnp.sum(gram_matrix * gram_matrix))
    scaled = gram_matrix / frobenius
    inverse_root = identity
    for repeat in range(NS_ITERS):
        factor = 1.5 * identity - 0.5 * jnp.dot(inverse_root, scaled, precision=lax.Precision.HIGHEST)
        scaled = jnp.dot(scaled, factor, precision=lax.Precision.HIGHEST)
        inverse_root = jnp.dot(factor, inverse_root, precision=lax.Precision.HIGHEST)
    mixing = inverse_root.astype(jnp.bfloat16)

    def rotate_domain(field):
        return jnp.dot(mixing.T, field, preferred_element_type=jnp.float32).astype(jnp.bfloat16)
    rotated = lax.map(rotate_domain, current)
    return rotated.transpose(1, 0, 2).reshape(S, NODES_ALL)
```

```python
import functools

import jax
import jax.numpy as jnp
from jax import lax
from jax.experimental import pallas as pl
from jax.experimental.pallas import tpu as pltpu
from jax.sharding import PartitionSpec as P

CHEB = 4
NS_ITERS = 5
GROUP = 4
VMEM_LIMIT = 56 * 1024 * 1024


def params():
    return pltpu.CompilerParams(vmem_limit_bytes=VMEM_LIMIT)


def vmem():
    return pl.BlockSpec(memory_space=pltpu.VMEM)


def smem():
    return pl.BlockSpec(memory_space=pltpu.SMEM)


def operators_kernel(node_total, counts_ref, conn_ref, pot_ref, kinetic_ref, ops_ref, diag_ref, ext):
    group, _, width = conn_ref.shape
    step = 3 * width // 4
    first = pl.program_id(0) * group

    @pl.when(pl.program_id(0) == 0)
    def _():
        ext[...] = jnp.zeros_like(ext)

    for j in range(group):
        cell = first + j
        slots = conn_ref[j] - cell * step
        slots = jnp.where(slots < 0, slots + node_total, slots)
        hit = lax.broadcasted_iota(jnp.int32, (width, width), 0) == slots
        perm = jnp.where(hit, 1.0, 0.0).astype(jnp.bfloat16)
        rows = jnp.dot(perm, kinetic_ref[...], preferred_element_type=jnp.float32)
        ops_ref[j] = lax.dot_general(
            rows.astype(jnp.bfloat16), perm, (((1,), (1,)), ((), ())),
            preferred_element_type=jnp.float32,
        ).astype(jnp.bfloat16)
        alive = jnp.where(cell < counts_ref[0], 1.0, 0.0)
        column = jnp.sum(jnp.where(hit, pot_ref[j] * alive, 0.0), axis=1, keepdims=True)
        span = pl.ds(pl.multiple_of(cell * step, 128), width)
        ext[span, :] = ext[span, :] + column

    @pl.when(pl.program_id(0) == pl.num_programs(0) - 1)
    def _():
        tail = width - step
        diag_ref[...] = ext[:node_total]
        diag_ref[:tail] = ext[:tail] + ext[node_total:]


def operators(connectivity, cell_kinetic, cell_potential, cell_counts, node_total):
    cells, width = connectivity.shape
    tail = width // 4
    return pl.pallas_call(
        functools.partial(operators_kernel, node_total),
        grid=(cells // GROUP,),
        in_specs=[
            smem(),
            pl.BlockSpec((GROUP, 1, width), lambda g: (g, 0, 0)),
            pl.BlockSpec((GROUP, 1, width), lambda g: (g, 0, 0)),
            pl.BlockSpec((width, width), lambda g: (0, 0)),
        ],
        out_specs=[
            pl.BlockSpec((GROUP, width, width), lambda g: (g, 0, 0)),
            pl.BlockSpec((node_total, 1), lambda g: (0, 0)),
        ],
        out_shape=[
            jax.ShapeDtypeStruct((cells, width, width), jnp.bfloat16),
            jax.ShapeDtypeStruct((node_total, 1), jnp.float32),
        ],
        scratch_shapes=[pltpu.VMEM((node_total + tail, 1), jnp.float32)],
        compiler_params=params(),
        name="window_operators",
    )(cell_counts, connectivity[:, None], cell_potential[:, None], cell_kinetic)


CHUNK = 16


def add_faces(faces_ref, halo, total):
    shared = faces_ref.shape[1]
    for side in range(2):

        def visit(i, carry, side=side):
            base = i * CHUNK
            nodes = [faces_ref[side, base + j] for j in range(CHUNK)]
            rows = [total[pl.ds(nodes[j], 1), :] for j in range(CHUNK)]
            gains = halo[pl.ds(pl.multiple_of(side * shared + base, CHUNK), CHUNK), :]
            for j in range(CHUNK):
                total[pl.ds(nodes[j], 1), :] = rows[j] + gains[j : j + 1]
            return carry

        lax.fori_loop(0, shared // CHUNK, visit, 0)


def pick_faces(faces_ref, total, halo):
    shared = faces_ref.shape[1]
    for side in range(2):

        def visit(i, carry, side=side):
            base = i * CHUNK
            nodes = [faces_ref[side, base + j] for j in range(CHUNK)]
            rows = [total[pl.ds(nodes[j], 1), :] for j in range(CHUNK)]
            halo[pl.ds(pl.multiple_of(side * shared + base, CHUNK), CHUNK), :] = jnp.concatenate(
                rows, axis=0
            )
            return carry

        lax.fori_loop(0, shared // CHUNK, visit, 0)


def unpack_halo(packed_refs, halo):
    for side, packed in enumerate(packed_refs):
        half, lanes = packed.shape
        base = side * 2 * half
        halo[base : base + half] = packed[:, : lanes // 2]
        halo[base + half : base + 2 * half] = packed[:, lanes // 2 :]


def pack_halo(halo, packed_refs):
    for side, packed in enumerate(packed_refs):
        half = packed.shape[0]
        base = side * 2 * half
        packed[...] = jnp.concatenate(
            [halo[base : base + half], halo[base + half : base + 2 * half]], axis=1
        )


ROWS = 768


def by_rows(total, visit):
    def step(i, carry):
        visit(pl.ds(pl.multiple_of(i * ROWS, ROWS), ROWS))
        return carry

    lax.fori_loop(0, total // ROWS, step, 0)


def apply_cells(counts_ref, scale_ref, ops_ref, field, ext):
    group, width, _ = ops_ref.shape
    step = 3 * width // 4
    for j in range(group):
        cell = pl.program_id(0) * group + j
        span = pl.ds(pl.multiple_of(cell * step, 128), width)
        scale = jnp.where(cell < counts_ref[0], scale_ref[cell], 0.0)
        product = jnp.dot(ops_ref[j], field[span, :], preferred_element_type=jnp.float32)
        ext[span, :] = ext[span, :] + product * scale


def apply_tail(faces_ref, local_ref, left_ref, right_ref, ext, halo):
    nodes = local_ref.shape[0]
    tail = ext.shape[0] - nodes
    ext[:tail] = ext[:tail] + ext[nodes:]
    pick_faces(faces_ref, ext, halo)
    pack_halo(halo, (left_ref, right_ref))

    def emit(rows):
        local_ref[rows, :] = ext[rows, :]

    by_rows(nodes, emit)


def first_kernel(counts_ref, scale_ref, faces_ref, ops_ref, diag_ref, states_ref,
                 local_ref, left_ref, right_ref, field, ext, halo):
    nodes = local_ref.shape[0]
    tail = ext.shape[0] - nodes

    @pl.when(pl.program_id(0) == 0)
    def _():
        def load(rows):
            value = states_ref[rows, :]
            field[rows, :] = value
            ext[rows, :] = value.astype(jnp.float32) * diag_ref[rows, :]

        by_rows(nodes, load)
        field[nodes:] = field[:tail]
        ext[nodes:] = jnp.zeros((tail, ext.shape[1]), jnp.float32)

    apply_cells(counts_ref, scale_ref, ops_ref, field, ext)

    @pl.when(pl.program_id(0) == pl.num_programs(0) - 1)
    def _():
        apply_tail(faces_ref, local_ref, left_ref, right_ref, ext, halo)


def next_kernel(twice, counts_ref, scale_ref, faces_ref, ops_ref, diag_ref, prev_ref, old_ref,
                from_left, from_right,
                local_ref, left_ref, right_ref, field_ref, field, ext, halo):
    nodes = local_ref.shape[0]
    tail = ext.shape[0] - nodes

    @pl.when(pl.program_id(0) == 0)
    def _():
        def load(rows):
            ext[rows, :] = old_ref[rows, :]

        by_rows(nodes, load)
        unpack_halo((from_left, from_right), halo)
        add_faces(faces_ref, halo, ext)

        def combine(rows):
            value = ext[rows, :]
            if twice:
                value = 2.0 * value - prev_ref[rows, :].astype(jnp.float32)
            value = value.astype(jnp.bfloat16)
            field[rows, :] = value
            field_ref[rows, :] = value
            ext[rows, :] = value.astype(jnp.float32) * diag_ref[rows, :]

        by_rows(nodes, combine)
        field[nodes:] = field[:tail]
        ext[nodes:] = jnp.zeros((tail, ext.shape[1]), jnp.float32)

    apply_cells(counts_ref, scale_ref, ops_ref, field, ext)

    @pl.when(pl.program_id(0) == pl.num_programs(0) - 1)
    def _():
        apply_tail(faces_ref, local_ref, left_ref, right_ref, ext, halo)


def last_kernel(faces_ref, prev_ref, old_ref, from_left, from_right, field_ref, ext, halo):
    nodes = old_ref.shape[0]

    def load(rows):
        ext[rows, :] = old_ref[rows, :]

    by_rows(nodes, load)
    unpack_halo((from_left, from_right), halo)
    add_faces(faces_ref, halo, ext)

    def combine(i, carry):
        rows = pl.ds(pl.multiple_of(i * 128, 128), 128)
        value = 2.0 * ext[rows, :] - prev_ref[rows, :].astype(jnp.float32)
        field_ref[:, rows] = value.T.astype(jnp.bfloat16)
        return carry

    lax.fori_loop(0, nodes // 128, combine, 0)


def newton(gram_matrix):
    identity = jnp.eye(gram_matrix.shape[0], dtype=jnp.float32)
    frobenius = jnp.sqrt(jnp.sum(gram_matrix * gram_matrix))
    scaled = gram_matrix / frobenius
    inverse_root = identity
    for repeat in range(NS_ITERS):
        factor = 1.5 * identity - 0.5 * jnp.dot(
            inverse_root, scaled, precision=lax.Precision.HIGHEST
        )
        scaled = jnp.dot(scaled, factor, precision=lax.Precision.HIGHEST)
        inverse_root = jnp.dot(factor, inverse_root, precision=lax.Precision.HIGHEST)
    return inverse_root.astype(jnp.bfloat16)


def newton_kernel(gram_ref, mixing_ref):
    mixing_ref[...] = newton(gram_ref[...])


def newton_call(gram_matrix):
    return pl.pallas_call(
        newton_kernel,
        in_specs=[vmem()],
        out_specs=vmem(),
        out_shape=jax.ShapeDtypeStruct(gram_matrix.shape, jnp.bfloat16),
        compiler_params=params(),
        name="newton",
    )(gram_matrix)


def body(states, cell_kinetic, cell_scale, cell_potential, connectivity, shared_nodes, cell_counts):
    domain = lax.axis_index("dom")
    domains = lax.axis_size("dom")
    state_rows, node_total = states.shape
    cells, width = connectivity.shape
    faces = shared_nodes[0]
    shared = faces.shape[1]
    tail = width // 4
    ops, diag = operators(connectivity, cell_kinetic, cell_potential, cell_counts, node_total)

    up = [(i, i + 1) for i in range(domains - 1)]
    down = [(i + 1, i) for i in range(domains - 1)]
    field_shape = jax.ShapeDtypeStruct((node_total, state_rows), jnp.bfloat16)
    outs = [
        jax.ShapeDtypeStruct((node_total, state_rows), jnp.float32),
        jax.ShapeDtypeStruct((shared // 2, 2 * state_rows), jnp.float32),
        jax.ShapeDtypeStruct((shared // 2, 2 * state_rows), jnp.float32),
    ]
    scratch = [
        pltpu.VMEM((node_total + tail, state_rows), jnp.bfloat16),
        pltpu.VMEM((node_total + tail, state_rows), jnp.float32),
        pltpu.VMEM((2 * shared, state_rows), jnp.float32),
    ]
    ops_spec = pl.BlockSpec((GROUP, width, width), lambda g: (g, 0, 0))

    def exchange(left, right):
        return (lax.ppermute(right, "dom", up), lax.ppermute(left, "dom", down))

    local, left, right = pl.pallas_call(
        first_kernel,
        grid=(cells // GROUP,),
        in_specs=[smem(), smem(), smem(), ops_spec, vmem(), vmem()],
        out_specs=[vmem()] * 3,
        out_shape=outs,
        scratch_shapes=scratch,
        compiler_params=params(),
        name="apply_first",
    )(cell_counts, cell_scale, faces, ops, diag, states.T)
    previous = states.T
    current = None
    for k in range(1, CHEB):
        halo = exchange(left, right)
        local, left, right, field = pl.pallas_call(
            functools.partial(next_kernel, k > 1),
            grid=(cells // GROUP,),
            in_specs=[smem(), smem(), smem(), ops_spec] + [vmem()] * 5,
            out_specs=[vmem()] * 4,
            out_shape=outs + [field_shape],
            scratch_shapes=scratch,
            compiler_params=params(),
            name="apply_next",
        )(cell_counts, cell_scale, faces, ops, diag, previous, local, *halo)
        if k > 1:
            previous = current
        current = field
    halo = exchange(left, right)
    filtered = pl.pallas_call(
        last_kernel,
        in_specs=[smem()] + [vmem()] * 4,
        out_specs=vmem(),
        out_shape=jax.ShapeDtypeStruct((state_rows, node_total), jnp.bfloat16),
        scratch_shapes=[
            pltpu.VMEM((node_total, state_rows), jnp.float32),
            pltpu.VMEM((2 * shared, state_rows), jnp.float32),
        ],
        compiler_params=params(),
        name="finish",
    )(faces, previous, local, *halo)

    row_shard = lax.all_to_all(filtered, "band", split_axis=1, concat_axis=0, tiled=True)
    piece_nodes = row_shard.shape[1]
    nodes = lax.axis_index("band") * piece_nodes + jnp.arange(piece_nodes, dtype=jnp.int32)
    has_left = (domain > 0).astype(jnp.float32)
    has_right = (domain < domains - 1).astype(jnp.float32)
    on_left = jnp.sum((nodes[None, :] == faces[0][:, None]).astype(jnp.float32), axis=0)
    on_right = jnp.sum((nodes[None, :] == faces[1][:, None]).astype(jnp.float32), axis=0)
    weight = (1.0 / (1.0 + has_left * on_left + has_right * on_right)).astype(jnp.bfloat16)
    weighted = row_shard * weight[None]
    partial_gram = lax.dot_general(
        weighted, row_shard, (((1,), (1,)), ((), ())), preferred_element_type=jnp.float32
    )
    gram_matrix = lax.psum(partial_gram, ("dom", "band"))
    mixing = newton_call(gram_matrix)
    rotated = lax.dot_general(
        mixing, row_shard, (((0,), (0,)), ((), ())), preferred_element_type=jnp.float32
    ).astype(jnp.bfloat16)
    return lax.all_to_all(rotated, "band", split_axis=0, concat_axis=1, tiled=True)


def solution(mesh):
    in_specs = (
        P("band", "dom"),
        P(),
        P("dom"),
        P("dom", None),
        P("dom", None),
        P("dom", None, None),
        P("dom"),
    )
    out_specs = P("band", "dom")
    return jax.shard_map(body, mesh=mesh, in_specs=in_specs, out_specs=out_specs, check_vma=False)
```

```python
import functools

import jax
import jax.numpy as jnp
from jax import lax
from jax.experimental import pallas as pl
from jax.experimental.pallas import tpu as pltpu
from jax.sharding import PartitionSpec as P

CHEB = 4
NS_ITERS = 5
GROUP = 4
VMEM_LIMIT = 56 * 1024 * 1024


def params():
    return pltpu.CompilerParams(vmem_limit_bytes=VMEM_LIMIT)


def vmem():
    return pl.BlockSpec(memory_space=pltpu.VMEM)


def smem():
    return pl.BlockSpec(memory_space=pltpu.SMEM)


def operators_kernel(node_total, counts_ref, conn_ref, pot_ref, kinetic_ref, ops_ref, diag_ref, ext):
    group, _, width = conn_ref.shape
    step = 3 * width // 4
    first = pl.program_id(0) * group

    @pl.when(pl.program_id(0) == 0)
    def _():
        ext[...] = jnp.zeros_like(ext)

    for j in range(group):
        cell = first + j
        slots = conn_ref[j] - cell * step
        slots = jnp.where(slots < 0, slots + node_total, slots)
        hit = lax.broadcasted_iota(jnp.int32, (width, width), 0) == slots
        perm = jnp.where(hit, 1.0, 0.0).astype(jnp.bfloat16)
        rows = jnp.dot(perm, kinetic_ref[...], preferred_element_type=jnp.float32)
        ops_ref[j] = lax.dot_general(
            rows.astype(jnp.bfloat16), perm, (((1,), (1,)), ((), ())),
            preferred_element_type=jnp.float32,
        ).astype(jnp.bfloat16)
        alive = jnp.where(cell < counts_ref[0], 1.0, 0.0)
        column = jnp.sum(jnp.where(hit, pot_ref[j] * alive, 0.0), axis=1, keepdims=True)
        span = pl.ds(pl.multiple_of(cell * step, 128), width)
        ext[span, :] = ext[span, :] + column

    @pl.when(pl.program_id(0) == pl.num_programs(0) - 1)
    def _():
        tail = width - step
        half, lanes = diag_ref.shape
        ext[:tail] = ext[:tail] + ext[node_total:]
        low = lax.broadcasted_iota(jnp.int32, (ROWS, lanes), 1) < lanes // 2
        for i in range(half // ROWS):
            diag_ref[i * ROWS : (i + 1) * ROWS] = jnp.where(
                low, ext[i * ROWS : (i + 1) * ROWS], ext[half + i * ROWS : half + (i + 1) * ROWS]
            )


def operators(connectivity, cell_kinetic, cell_potential, cell_counts, node_total, state_rows):
    cells, width = connectivity.shape
    tail = width // 4
    return pl.pallas_call(
        functools.partial(operators_kernel, node_total),
        grid=(cells // GROUP,),
        in_specs=[
            smem(),
            pl.BlockSpec((GROUP, 1, width), lambda g: (g, 0, 0)),
            pl.BlockSpec((GROUP, 1, width), lambda g: (g, 0, 0)),
            pl.BlockSpec((width, width), lambda g: (0, 0)),
        ],
        out_specs=[
            pl.BlockSpec((GROUP, width, width), lambda g: (g, 0, 0)),
            pl.BlockSpec((node_total // 2, 2 * state_rows), lambda g: (0, 0)),
        ],
        out_shape=[
            jax.ShapeDtypeStruct((cells, width, width), jnp.bfloat16),
            jax.ShapeDtypeStruct((node_total // 2, 2 * state_rows), jnp.float32),
        ],
        scratch_shapes=[pltpu.VMEM((node_total + tail, 1), jnp.float32)],
        compiler_params=params(),
        name="window_operators",
    )(cell_counts, connectivity[:, None], cell_potential[:, None], cell_kinetic)


CHUNK = 16


ROWS = 768


def by_rows(total, visit):
    def step(i, carry):
        visit(pl.multiple_of(i * ROWS, ROWS))
        return carry

    lax.fori_loop(0, total // ROWS, step, 0)


def swap_halves(value):
    lanes = value.shape[1]
    return jnp.concatenate([value[:, lanes // 2 :], value[:, : lanes // 2]], axis=1)


def add_faces(sides_ref, faces_ref, from_refs, halo, total):
    shared = faces_ref.shape[1]
    for side, packed in enumerate(from_refs):
        half, lanes = packed.shape
        base = side * shared
        rows = jnp.where(sides_ref[side] > 0, packed[...].astype(jnp.float32), 0.0)
        halo[base : base + half] = rows[:, : lanes // 2]
        halo[base + half : base + shared] = rows[:, lanes // 2 :]
    for side in range(2):

        def visit(i, carry, side=side):
            base = i * CHUNK
            nodes = [faces_ref[side, base + j] for j in range(CHUNK)]
            gains = [halo[pl.ds(side * shared + base + j, 1), :] for j in range(CHUNK)]
            rows = [total[pl.ds(nodes[j], 1), :] + gains[j] for j in range(CHUNK)]
            for j in range(CHUNK):
                total[pl.ds(nodes[j], 1), :] = rows[j]
            return carry

        lax.fori_loop(0, shared // CHUNK, visit, 0)


def pick_faces(faces_ref, nodes_ref, ext, half_nodes, picked, to_refs):
    shared = faces_ref.shape[1]
    half = shared // 2
    for side in range(2):

        def visit(i, carry, side=side):
            base = i * CHUNK
            nodes = [faces_ref[side, base + j] for j in range(CHUNK)]
            spots = [jnp.where(n >= half_nodes, n - half_nodes, n) for n in nodes]
            rows = [ext[pl.ds(spot, 1), :] for spot in spots]
            for j in range(CHUNK):
                picked[pl.ds(side * shared + base + j, 1), :] = rows[j]
            return carry

        lax.fori_loop(0, shared // CHUNK, visit, 0)
        base = side * shared
        lanes = picked.shape[1]
        low = lax.broadcasted_iota(jnp.int32, (half, lanes), 1) < lanes // 2
        first, second = picked[base : base + half], picked[base + half : base + shared]
        upper_first = nodes_ref[base : base + half] >= half_nodes
        upper_second = nodes_ref[base + half : base + shared] >= half_nodes
        first = jnp.where(upper_first, swap_halves(first), first)
        second = jnp.where(upper_second, second, swap_halves(second))
        to_refs[side][...] = jnp.where(low, first, second).astype(to_refs[side].dtype)


def apply_cells(counts_ref, scale_ref, low_ops, high_ops, field, ext):
    group, width, _ = low_ops.shape
    step = 3 * width // 4
    lanes = ext.shape[1]
    low = lax.broadcasted_iota(jnp.int32, (1, lanes), 1) < lanes // 2
    for j in range(group):
        cell = pl.program_id(0) * group + j
        upper = cell + pl.num_programs(0) * group
        span = pl.ds(pl.multiple_of(cell * step, 128), width)
        scale = jnp.where(cell < counts_ref[0], scale_ref[cell], 0.0)
        upper_scale = jnp.where(upper < counts_ref[0], scale_ref[upper], 0.0)
        window = field[span, :]
        first = jnp.dot(low_ops[j], window, preferred_element_type=jnp.float32)
        second = jnp.dot(high_ops[j], window, preferred_element_type=jnp.float32)
        ext[span, :] = ext[span, :] + jnp.where(low, first * scale, second * upper_scale)


def finish_cells(faces_ref, nodes_ref, local_ref, left_ref, right_ref, ext, picked):
    half = local_ref.shape[0]
    tail = ext.shape[0] - half
    ext[:tail] = ext[:tail] + swap_halves(ext[half:])
    pick_faces(faces_ref, nodes_ref, ext, half, picked, (left_ref, right_ref))

    def emit(base):
        local_ref[pl.ds(base, ROWS), :] = ext[pl.ds(base, ROWS), :]

    by_rows(half, emit)


def start_tail(field, ext, half):
    tail = ext.shape[0] - half
    field[half:] = swap_halves(field[:tail])
    ext[half:] = jnp.zeros((tail, ext.shape[1]), jnp.float32)


def first_kernel(counts_ref, scale_ref, faces_ref, nodes_ref, low_ops, high_ops, diag_ref,
                 states_ref, local_ref, left_ref, right_ref, field_ref, field, ext, picked):
    half = local_ref.shape[0]

    @pl.when(pl.program_id(0) == 0)
    def _():
        def load(i, carry):
            low = pl.ds(pl.multiple_of(i * 128, 128), 128)
            high = pl.ds(pl.multiple_of(half + i * 128, 128), 128)
            pair = jnp.concatenate([states_ref[:, low], states_ref[:, high]], axis=0)
            value = pair.astype(jnp.float32).T
            rounded = value.astype(jnp.bfloat16)
            field[low, :] = rounded
            field_ref[low, :] = rounded
            ext[low, :] = value * diag_ref[low, :]
            return carry

        lax.fori_loop(0, half // 128, load, 0)
        start_tail(field, ext, half)

    apply_cells(counts_ref, scale_ref, low_ops, high_ops, field, ext)

    @pl.when(pl.program_id(0) == pl.num_programs(0) - 1)
    def _():
        finish_cells(faces_ref, nodes_ref, local_ref, left_ref, right_ref, ext, picked)


def unpack_local(old_ref, total):
    half, lanes = old_ref.shape

    def load(base):
        value = old_ref[pl.ds(base, ROWS), :]
        total[pl.ds(base, ROWS), :] = value[:, : lanes // 2]
        total[pl.ds(half + base, ROWS), :] = value[:, lanes // 2 :]

    by_rows(half, load)


def next_kernel(twice, counts_ref, scale_ref, faces_ref, sides_ref, nodes_ref, low_ops, high_ops,
                diag_ref, prev_ref, old_ref, from_left, from_right,
                local_ref, left_ref, right_ref, field_ref, field, ext, picked, total, halo):
    half = local_ref.shape[0]

    @pl.when(pl.program_id(0) == 0)
    def _():
        unpack_local(old_ref, total)
        add_faces(sides_ref, faces_ref, (from_left, from_right), halo, total)

        def combine(base):
            rows = pl.ds(base, ROWS)
            value = jnp.concatenate([total[rows, :], total[pl.ds(half + base, ROWS), :]], axis=1)
            if twice:
                value = 2.0 * value - prev_ref[rows, :].astype(jnp.float32)
            value = value.astype(jnp.bfloat16)
            field[rows, :] = value
            field_ref[rows, :] = value
            ext[rows, :] = value.astype(jnp.float32) * diag_ref[rows, :]

        by_rows(half, combine)
        start_tail(field, ext, half)

    apply_cells(counts_ref, scale_ref, low_ops, high_ops, field, ext)

    @pl.when(pl.program_id(0) == pl.num_programs(0) - 1)
    def _():
        finish_cells(faces_ref, nodes_ref, local_ref, left_ref, right_ref, ext, picked)


def last_kernel(faces_ref, sides_ref, prev_ref, old_ref, from_left, from_right, field_ref,
                total, halo):
    half, lanes = old_ref.shape
    unpack_local(old_ref, total)
    add_faces(sides_ref, faces_ref, (from_left, from_right), halo, total)

    def combine(i, carry):
        low = pl.ds(pl.multiple_of(i * 128, 128), 128)
        high = pl.ds(pl.multiple_of(half + i * 128, 128), 128)
        value = jnp.concatenate([total[low, :], total[high, :]], axis=1)
        value = (2.0 * value - prev_ref[low, :].astype(jnp.float32)).T
        field_ref[:, low] = value[: lanes // 2].astype(jnp.bfloat16)
        field_ref[:, high] = value[lanes // 2 :].astype(jnp.bfloat16)
        return carry

    lax.fori_loop(0, half // 128, combine, 0)


def exchange_kernel(domains, left_ref, right_ref, from_left, from_right,
                    send_up, send_down, recv_up, recv_down):
    dom, band = lax.axis_index("dom"), lax.axis_index("band")
    barrier = pltpu.get_barrier_semaphore()
    has_left, has_right = dom > 0, dom < domains - 1

    @pl.when(has_left)
    def _():
        pl.semaphore_signal(barrier, inc=1, device_id=(dom - 1, band), device_id_type=MESH)

    @pl.when(has_right)
    def _():
        pl.semaphore_signal(barrier, inc=1, device_id=(dom + 1, band), device_id_type=MESH)

    pl.semaphore_wait(barrier, jnp.where(has_left & has_right, 2, 1))

    down = pltpu.make_async_remote_copy(
        src_ref=left_ref, dst_ref=from_right, send_sem=send_down, recv_sem=recv_down,
        device_id=(dom - 1, band), device_id_type=MESH)
    up = pltpu.make_async_remote_copy(
        src_ref=right_ref, dst_ref=from_left, send_sem=send_up, recv_sem=recv_up,
        device_id=(dom + 1, band), device_id_type=MESH)

    @pl.when(has_left)
    def _():
        down.start()

    @pl.when(has_right)
    def _():
        up.start()

    @pl.when(has_left)
    def _():
        down.wait_send()
        up.wait_recv()

    @pl.when(has_right)
    def _():
        up.wait_send()
        down.wait_recv()


def exchange(left, right):
    anywhere = pl.BlockSpec(memory_space=pl.ANY)
    return pl.pallas_call(
        functools.partial(exchange_kernel, lax.axis_size("dom")),
        in_specs=[anywhere] * 2,
        out_specs=[anywhere] * 2,
        out_shape=[jax.ShapeDtypeStruct(left.shape, left.dtype)] * 2,
        scratch_shapes=[pltpu.SemaphoreType.DMA] * 4,
        compiler_params=pltpu.CompilerParams(collective_id=1, has_side_effects=True),
        name="exchange",
    )(left, right)


def newton(gram_matrix):
    identity = jnp.eye(gram_matrix.shape[0], dtype=jnp.float32)
    frobenius = jnp.sqrt(jnp.sum(gram_matrix * gram_matrix))
    scaled = gram_matrix / frobenius
    inverse_root = identity
    for repeat in range(NS_ITERS):
        factor = 1.5 * identity - 0.5 * jnp.dot(
            inverse_root, scaled, precision=lax.Precision.HIGHEST
        )
        scaled = jnp.dot(scaled, factor, precision=lax.Precision.HIGHEST)
        inverse_root = jnp.dot(factor, inverse_root, precision=lax.Precision.HIGHEST)
    return inverse_root.astype(jnp.bfloat16)


MESH = pl.DeviceIdType.MESH


def gram_kernel(domains, bands, part_ref, mixing_ref, from_dom, from_band, total,
                send_dom, recv_dom, send_band, recv_band, send_back, recv_back):
    dom, band = lax.axis_index("dom"), lax.axis_index("band")
    rows = part_ref.shape[0] // domains

    def dom_peer(i):
        return (lax.rem(dom + i, domains), band)

    def band_peer(i):
        return (dom, lax.rem(band + i, bands))

    peers = [dom_peer(i) for i in range(1, domains)] + [band_peer(i) for i in range(1, bands)]
    barrier = pltpu.get_barrier_semaphore()
    for peer in peers:
        pl.semaphore_signal(barrier, inc=1, device_id=peer, device_id_type=MESH)
    pl.semaphore_wait(barrier, len(peers))

    def span(index):
        return pl.ds(pl.multiple_of(index * rows, 8), rows)

    scatter = []
    for i in range(1, domains):
        peer = dom_peer(i)
        scatter.append(pltpu.make_async_remote_copy(
            src_ref=part_ref.at[span(peer[0])], dst_ref=from_dom.at[i],
            send_sem=send_dom.at[i], recv_sem=recv_dom.at[i],
            device_id=peer, device_id_type=MESH))
    for copy in scatter:
        copy.start()
    own = part_ref[span(dom), :]
    for copy in scatter:
        copy.wait()
    for i in range(1, domains):
        own = own + from_dom[i]
    from_band[band] = own
    across = []
    for i in range(1, bands):
        across.append(pltpu.make_async_remote_copy(
            src_ref=from_band.at[band], dst_ref=from_band.at[band],
            send_sem=send_band.at[i], recv_sem=recv_band.at[i],
            device_id=band_peer(i), device_id_type=MESH))
    for copy in across:
        copy.start()
    for copy in across:
        copy.wait()
    summed = from_band[0]
    for i in range(1, bands):
        summed = summed + from_band[i]
    total[span(dom), :] = summed
    back = []
    for i in range(1, domains):
        back.append(pltpu.make_async_remote_copy(
            src_ref=total.at[span(dom)], dst_ref=total.at[span(dom)],
            send_sem=send_back.at[i], recv_sem=recv_back.at[i],
            device_id=dom_peer(i), device_id_type=MESH))
    for copy in back:
        copy.start()
    for copy in back:
        copy.wait()
    mixing_ref[...] = newton(total[...])


def gram_call(partial_gram):
    domains, bands = lax.axis_size("dom"), lax.axis_size("band")
    size = partial_gram.shape[0]
    rows = size // domains
    return pl.pallas_call(
        functools.partial(gram_kernel, domains, bands),
        in_specs=[vmem()],
        out_specs=vmem(),
        out_shape=jax.ShapeDtypeStruct((size, size), jnp.bfloat16),
        scratch_shapes=[
            pltpu.VMEM((domains, rows, size), jnp.float32),
            pltpu.VMEM((bands, rows, size), jnp.float32),
            pltpu.VMEM((size, size), jnp.float32),
            pltpu.SemaphoreType.DMA((domains,)),
            pltpu.SemaphoreType.DMA((domains,)),
            pltpu.SemaphoreType.DMA((bands,)),
            pltpu.SemaphoreType.DMA((bands,)),
            pltpu.SemaphoreType.DMA((domains,)),
            pltpu.SemaphoreType.DMA((domains,)),
        ],
        compiler_params=pltpu.CompilerParams(
            vmem_limit_bytes=VMEM_LIMIT, collective_id=0, has_side_effects=True
        ),
        name="gram_newton",
    )(partial_gram)


def body(states, cell_kinetic, cell_scale, cell_potential, connectivity, shared_nodes, cell_counts):
    domain = lax.axis_index("dom")
    domains = lax.axis_size("dom")
    state_rows, node_total = states.shape
    cells, width = connectivity.shape
    faces = shared_nodes[0]
    shared = faces.shape[1]
    tail = width // 4
    half = node_total // 2
    lanes = 2 * state_rows
    ops, diag = operators(
        connectivity, cell_kinetic, cell_potential, cell_counts, node_total, state_rows
    )
    sides = jnp.stack([domain > 0, domain < domains - 1]).astype(jnp.int32)
    face_nodes = faces.reshape(2 * shared, 1)

    field_shape = jax.ShapeDtypeStruct((half, lanes), jnp.bfloat16)
    outs = [
        jax.ShapeDtypeStruct((half, lanes), jnp.float32),
        jax.ShapeDtypeStruct((shared // 2, lanes), jnp.bfloat16),
        jax.ShapeDtypeStruct((shared // 2, lanes), jnp.bfloat16),
        field_shape,
    ]
    scratch = [
        pltpu.VMEM((half + tail, lanes), jnp.bfloat16),
        pltpu.VMEM((half + tail, lanes), jnp.float32),
        pltpu.VMEM((2 * shared, lanes), jnp.float32),
    ]
    total_scratch = [
        pltpu.VMEM((node_total, state_rows), jnp.float32),
        pltpu.VMEM((2 * shared, state_rows), jnp.float32),
    ]
    group = GROUP // 2
    steps = cells // GROUP
    ops_specs = [
        pl.BlockSpec((group, width, width), lambda g: (g, 0, 0)),
        pl.BlockSpec((group, width, width), lambda g: (g + steps, 0, 0)),
    ]
    local, left, right, previous = pl.pallas_call(
        first_kernel,
        grid=(steps,),
        in_specs=[smem()] * 3 + [vmem()] + ops_specs + [vmem()] * 2,
        out_specs=[vmem()] * 4,
        out_shape=outs,
        scratch_shapes=scratch,
        compiler_params=params(),
        name="apply_first",
    )(cell_counts, cell_scale, faces, face_nodes, ops, ops, diag, states)
    current = previous
    for k in range(1, CHEB):
        halo = exchange(left, right)
        local, left, right, field = pl.pallas_call(
            functools.partial(next_kernel, k > 1),
            grid=(steps,),
            in_specs=[smem()] * 4 + [vmem()] + ops_specs + [vmem()] * 5,
            out_specs=[vmem()] * 4,
            out_shape=outs,
            scratch_shapes=scratch + total_scratch,
            compiler_params=params(),
            name="apply_next",
        )(cell_counts, cell_scale, faces, sides, face_nodes, ops, ops, diag, previous, local, *halo)
        previous = current
        current = field
    halo = exchange(left, right)
    filtered = pl.pallas_call(
        last_kernel,
        in_specs=[smem()] * 2 + [vmem()] * 4,
        out_specs=vmem(),
        out_shape=jax.ShapeDtypeStruct((state_rows, node_total), jnp.bfloat16),
        scratch_shapes=total_scratch,
        compiler_params=params(),
        name="finish",
    )(faces, sides, previous, local, *halo)

    row_shard = lax.all_to_all(filtered, "band", split_axis=1, concat_axis=0, tiled=True)
    piece_nodes = row_shard.shape[1]
    nodes = lax.axis_index("band") * piece_nodes + jnp.arange(piece_nodes, dtype=jnp.int32)
    has_left = (domain > 0).astype(jnp.float32)
    has_right = (domain < domains - 1).astype(jnp.float32)
    on_left = jnp.sum((nodes[None, :] == faces[0][:, None]).astype(jnp.float32), axis=0)
    on_right = jnp.sum((nodes[None, :] == faces[1][:, None]).astype(jnp.float32), axis=0)
    weight = (1.0 / (1.0 + has_left * on_left + has_right * on_right)).astype(jnp.bfloat16)
    weighted = row_shard * weight[None]
    partial_gram = lax.dot_general(
        weighted, row_shard, (((1,), (1,)), ((), ())), preferred_element_type=jnp.float32
    )
    mixing = gram_call(partial_gram)
    rotated = lax.dot_general(
        mixing, row_shard, (((0,), (0,)), ((), ())), preferred_element_type=jnp.float32
    ).astype(jnp.bfloat16)
    return lax.all_to_all(rotated, "band", split_axis=0, concat_axis=1, tiled=True)


def solution(mesh):
    in_specs = (
        P("band", "dom"),
        P(),
        P("dom"),
        P("dom", None),
        P("dom", None),
        P("dom", None, None),
        P("dom"),
    )
    out_specs = P("band", "dom")
    return jax.shard_map(body, mesh=mesh, in_specs=in_specs, out_specs=out_specs, check_vma=False)
```

```python
import functools

import jax
import jax.numpy as jnp
from jax import lax
from jax.experimental import pallas as pl
from jax.experimental.pallas import tpu as pltpu
from jax.sharding import PartitionSpec as P

CHEB = 4
NS_ITERS = 5
GROUP = 4
VMEM_LIMIT = 56 * 1024 * 1024
MESH = pl.DeviceIdType.MESH


def params():
    return pltpu.CompilerParams(vmem_limit_bytes=VMEM_LIMIT)


def vmem():
    return pl.BlockSpec(memory_space=pltpu.VMEM)


def smem():
    return pl.BlockSpec(memory_space=pltpu.SMEM)


def operators_kernel(node_total, counts_ref, conn_ref, pot_ref, kinetic_ref, ops_ref, diag_ref, ext):
    group, width, _ = ops_ref.shape
    step = 3 * width // 4
    first = pl.program_id(0) * group

    @pl.when(pl.program_id(0) == 0)
    def _():
        ext[...] = jnp.zeros_like(ext)

    for j in range(group):
        cell = first + j
        slots = conn_ref[pl.ds(cell, 1), :] - cell * step
        slots = jnp.where(slots < 0, slots + node_total, slots)
        hit = lax.broadcasted_iota(jnp.int32, (width, width), 0) == slots
        perm = jnp.where(hit, 1.0, 0.0).astype(jnp.bfloat16)
        rows = jnp.dot(perm, kinetic_ref[...], preferred_element_type=jnp.float32)
        ops_ref[j] = lax.dot_general(
            rows.astype(jnp.bfloat16), perm, (((1,), (1,)), ((), ())),
            preferred_element_type=jnp.float32,
        ).astype(jnp.bfloat16)
        alive = jnp.where(cell < counts_ref[0], 1.0, 0.0)
        column = jnp.sum(jnp.where(hit, pot_ref[pl.ds(cell, 1), :] * alive, 0.0), axis=1, keepdims=True)
        span = pl.ds(pl.multiple_of(cell * step, 128), width)
        ext[span, :] = ext[span, :] + column

    @pl.when(pl.program_id(0) == pl.num_programs(0) - 1)
    def _():
        tail = width - step
        half, lanes = diag_ref.shape
        ext[:tail] = ext[:tail] + ext[node_total:]
        low = lax.broadcasted_iota(jnp.int32, (ROWS, lanes), 1) < lanes // 2
        for i in range(half // ROWS):
            diag_ref[i * ROWS : (i + 1) * ROWS] = jnp.where(
                low, ext[i * ROWS : (i + 1) * ROWS], ext[half + i * ROWS : half + (i + 1) * ROWS]
            )


def operators(connectivity, cell_kinetic, cell_potential, cell_counts, node_total, state_rows):
    cells, width = connectivity.shape
    tail = width // 4
    return pl.pallas_call(
        functools.partial(operators_kernel, node_total),
        grid=(cells // GROUP,),
        in_specs=[
            smem(),
            pl.BlockSpec((cells, width), lambda g: (0, 0)),
            pl.BlockSpec((cells, width), lambda g: (0, 0)),
            pl.BlockSpec((width, width), lambda g: (0, 0)),
        ],
        out_specs=[
            pl.BlockSpec((GROUP, width, width), lambda g: (g, 0, 0)),
            pl.BlockSpec((node_total // 2, 2 * state_rows), lambda g: (0, 0)),
        ],
        out_shape=[
            jax.ShapeDtypeStruct((cells, width, width), jnp.bfloat16),
            jax.ShapeDtypeStruct((node_total // 2, 2 * state_rows), jnp.float32),
        ],
        scratch_shapes=[pltpu.VMEM((node_total + tail, 1), jnp.float32)],
        compiler_params=params(),
        name="window_operators",
    )(cell_counts, connectivity, cell_potential, cell_kinetic)


ADD_CHUNK = 32
PICK_CHUNK = 64


ROWS = 768


def by_rows(total, visit):
    def step(i, carry):
        visit(pl.multiple_of(i * ROWS, ROWS))
        return carry

    lax.fori_loop(0, total // ROWS, step, 0)


def swap_halves(value):
    lanes = value.shape[1]
    return jnp.concatenate([value[:, lanes // 2 :], value[:, : lanes // 2]], axis=1)


def add_faces(sides_ref, faces_ref, from_refs, halo, total):
    shared = faces_ref.shape[1]
    for side, packed in enumerate(from_refs):
        half, lanes = packed.shape
        base = side * shared
        rows = jnp.where(sides_ref[side] > 0, packed[...].astype(jnp.float32), 0.0)
        halo[base : base + half] = rows[:, : lanes // 2]
        halo[base + half : base + shared] = rows[:, lanes // 2 :]
    for side in range(2):

        def visit(i, carry, side=side):
            base = i * ADD_CHUNK
            nodes = [faces_ref[side, base + j] for j in range(ADD_CHUNK)]
            gains = halo.at[pl.ds(pl.multiple_of(side * shared + base, ADD_CHUNK), ADD_CHUNK)]
            rows = [total[pl.ds(nodes[j], 1), :] + gains[j : j + 1, :] for j in range(ADD_CHUNK)]
            for j in range(ADD_CHUNK):
                total[pl.ds(nodes[j], 1), :] = rows[j]
            return carry

        lax.fori_loop(0, shared // ADD_CHUNK, visit, 0)


def pick_faces(spots_ref, nodes_ref, ext, half_nodes, picked, to_refs):
    shared = spots_ref.shape[1]
    half = shared // 2
    for side in range(2):

        def visit(i, carry, side=side):
            base = i * PICK_CHUNK
            block = picked.at[pl.ds(pl.multiple_of(side * shared + base, PICK_CHUNK), PICK_CHUNK)]
            for j in range(PICK_CHUNK):
                block[j : j + 1, :] = ext[pl.ds(spots_ref[side, base + j], 1), :]
            return carry

        lax.fori_loop(0, shared // PICK_CHUNK, visit, 0)
        base = side * shared
        lanes = picked.shape[1]
        low = lax.broadcasted_iota(jnp.int32, (half, lanes), 1) < lanes // 2
        first, second = picked[base : base + half], picked[base + half : base + shared]
        upper_first = nodes_ref[base : base + half] >= half_nodes
        upper_second = nodes_ref[base + half : base + shared] >= half_nodes
        first = jnp.where(upper_first, swap_halves(first), first)
        second = jnp.where(upper_second, second, swap_halves(second))
        to_refs[side][...] = jnp.where(low, first, second).astype(to_refs[side].dtype)


def apply_cells(counts_ref, scale_ref, low_ops, high_ops, field, ext):
    group, width, _ = low_ops.shape
    step = 3 * width // 4
    lanes = ext.shape[1]
    low = lax.broadcasted_iota(jnp.int32, (1, lanes), 1) < lanes // 2
    for j in range(group):
        cell = pl.program_id(0) * group + j
        upper = cell + pl.num_programs(0) * group
        span = pl.ds(pl.multiple_of(cell * step, 128), width)
        scale = jnp.where(cell < counts_ref[0], scale_ref[cell], 0.0)
        upper_scale = jnp.where(upper < counts_ref[0], scale_ref[upper], 0.0)
        window = field[span, :]
        first = jnp.dot(low_ops[j], window, preferred_element_type=jnp.float32)
        second = jnp.dot(high_ops[j], window, preferred_element_type=jnp.float32)
        ext[span, :] = ext[span, :] + jnp.where(low, first * scale, second * upper_scale)


def finish_cells(spots_ref, nodes_ref, local_ref, left_ref, right_ref, ext, picked):
    half = local_ref.shape[0]
    tail = ext.shape[0] - half
    ext[:tail] = ext[:tail] + swap_halves(ext[half:])
    pick_faces(spots_ref, nodes_ref, ext, half, picked, (left_ref, right_ref))

    def emit(base):
        local_ref[pl.ds(base, ROWS), :] = ext[pl.ds(base, ROWS), :]

    by_rows(half, emit)


def start_tail(field, ext, half):
    tail = ext.shape[0] - half
    field[half:] = swap_halves(field[:tail])
    ext[half:] = jnp.zeros((tail, ext.shape[1]), jnp.float32)


def first_kernel(counts_ref, scale_ref, spots_ref, nodes_ref, low_ops, high_ops, diag_ref,
                 states_ref, local_ref, left_ref, right_ref, field_ref, field, ext, picked):
    half = local_ref.shape[0]

    @pl.when(pl.program_id(0) == 0)
    def _():
        def load(i, carry):
            low = pl.ds(pl.multiple_of(i * 128, 128), 128)
            high = pl.ds(pl.multiple_of(half + i * 128, 128), 128)
            pair = jnp.concatenate([states_ref[:, low], states_ref[:, high]], axis=0)
            value = pair.astype(jnp.float32).T
            rounded = value.astype(jnp.bfloat16)
            field[low, :] = rounded
            field_ref[low, :] = rounded
            ext[low, :] = value * diag_ref[low, :]
            return carry

        lax.fori_loop(0, half // 128, load, 0)
        start_tail(field, ext, half)

    apply_cells(counts_ref, scale_ref, low_ops, high_ops, field, ext)

    @pl.when(pl.program_id(0) == pl.num_programs(0) - 1)
    def _():
        finish_cells(spots_ref, nodes_ref, local_ref, left_ref, right_ref, ext, picked)


def unpack_local(old_ref, total):
    half, lanes = old_ref.shape

    def load(base):
        value = old_ref[pl.ds(base, ROWS), :]
        total[pl.ds(base, ROWS), :] = value[:, : lanes // 2]
        total[pl.ds(half + base, ROWS), :] = value[:, lanes // 2 :]

    by_rows(half, load)


def next_kernel(twice, counts_ref, scale_ref, faces_ref, spots_ref, sides_ref, nodes_ref, low_ops, high_ops,
                diag_ref, prev_ref, old_ref, from_left, from_right,
                local_ref, left_ref, right_ref, field_ref, field, ext, picked, total, halo):
    half = local_ref.shape[0]

    @pl.when(pl.program_id(0) == 0)
    def _():
        unpack_local(old_ref, total)
        add_faces(sides_ref, faces_ref, (from_left, from_right), halo, total)

        def combine(base):
            rows = pl.ds(base, ROWS)
            value = jnp.concatenate([total[rows, :], total[pl.ds(half + base, ROWS), :]], axis=1)
            if twice:
                value = 2.0 * value - prev_ref[rows, :].astype(jnp.float32)
            value = value.astype(jnp.bfloat16)
            field[rows, :] = value
            field_ref[rows, :] = value
            ext[rows, :] = value.astype(jnp.float32) * diag_ref[rows, :]

        by_rows(half, combine)
        start_tail(field, ext, half)

    apply_cells(counts_ref, scale_ref, low_ops, high_ops, field, ext)

    @pl.when(pl.program_id(0) == pl.num_programs(0) - 1)
    def _():
        finish_cells(spots_ref, nodes_ref, local_ref, left_ref, right_ref, ext, picked)


def last_kernel(faces_ref, sides_ref, prev_ref, old_ref, from_left, from_right, field_ref,
                total, halo):
    half, lanes = old_ref.shape
    unpack_local(old_ref, total)
    add_faces(sides_ref, faces_ref, (from_left, from_right), halo, total)

    def combine(i, carry):
        low = pl.ds(pl.multiple_of(i * 128, 128), 128)
        high = pl.ds(pl.multiple_of(half + i * 128, 128), 128)
        value = jnp.concatenate([total[low, :], total[high, :]], axis=1)
        value = (2.0 * value - prev_ref[low, :].astype(jnp.float32)).T
        field_ref[:, low] = value[: lanes // 2].astype(jnp.bfloat16)
        field_ref[:, high] = value[lanes // 2 :].astype(jnp.bfloat16)
        return carry

    lax.fori_loop(0, half // 128, combine, 0)


def exchange_kernel(domains, left_ref, right_ref, from_left, from_right,
                    send_up, send_down, recv_up, recv_down):
    dom, band = lax.axis_index("dom"), lax.axis_index("band")
    barrier = pltpu.get_barrier_semaphore()
    has_left, has_right = dom > 0, dom < domains - 1

    @pl.when(has_left)
    def _():
        pl.semaphore_signal(barrier, inc=1, device_id=(dom - 1, band), device_id_type=MESH)

    @pl.when(has_right)
    def _():
        pl.semaphore_signal(barrier, inc=1, device_id=(dom + 1, band), device_id_type=MESH)

    pl.semaphore_wait(barrier, jnp.where(has_left & has_right, 2, 1))

    down = pltpu.make_async_remote_copy(
        src_ref=left_ref, dst_ref=from_right, send_sem=send_down, recv_sem=recv_down,
        device_id=(dom - 1, band), device_id_type=MESH)
    up = pltpu.make_async_remote_copy(
        src_ref=right_ref, dst_ref=from_left, send_sem=send_up, recv_sem=recv_up,
        device_id=(dom + 1, band), device_id_type=MESH)

    @pl.when(has_left)
    def _():
        down.start()

    @pl.when(has_right)
    def _():
        up.start()

    @pl.when(has_left)
    def _():
        down.wait_send()
        up.wait_recv()

    @pl.when(has_right)
    def _():
        up.wait_send()
        down.wait_recv()


def exchange(left, right):
    anywhere = pl.BlockSpec(memory_space=pl.ANY)
    return pl.pallas_call(
        functools.partial(exchange_kernel, lax.axis_size("dom")),
        in_specs=[anywhere] * 2,
        out_specs=[anywhere] * 2,
        out_shape=[jax.ShapeDtypeStruct(left.shape, left.dtype)] * 2,
        scratch_shapes=[pltpu.SemaphoreType.DMA] * 4,
        compiler_params=pltpu.CompilerParams(collective_id=1, has_side_effects=True),
        name="exchange",
    )(left, right)


def newton(gram_matrix):
    size = gram_matrix.shape[0]
    identity = (
        lax.broadcasted_iota(jnp.int32, (size, size), 0)
        == lax.broadcasted_iota(jnp.int32, (size, size), 1)
    ).astype(jnp.float32)
    frobenius = jnp.sqrt(jnp.sum(gram_matrix * gram_matrix))
    scaled = gram_matrix / frobenius
    inverse_root = None
    for repeat in range(NS_ITERS):
        if repeat == 0:
            factor = 1.5 * identity - 0.5 * scaled
            inverse_root = factor
        else:
            factor = 1.5 * identity - 0.5 * jnp.dot(
                inverse_root, scaled, precision=lax.Precision.HIGHEST
            )
            inverse_root = jnp.dot(factor, inverse_root, precision=lax.Precision.HIGHEST)
        if repeat < NS_ITERS - 1:
            scaled = jnp.dot(scaled, factor, precision=lax.Precision.HIGHEST)
    return inverse_root


def closing_kernel(domains, bands, filtered_ref, weight_ref, out_ref, shard, turned, mixing, part,
                   from_dom, from_band, total,
                   send_in, recv_in, send_out, recv_out,
                   send_dom, recv_dom, send_band, recv_band, send_back, recv_back):
    dom, band = lax.axis_index("dom"), lax.axis_index("band")
    rows = part.shape[0] // domains
    state_rows = filtered_ref.shape[0]
    piece = shard.shape[1]

    def dom_peer(i):
        return (lax.rem(dom + i, domains), band)

    def band_peer(i):
        return (dom, lax.rem(band + i, bands))

    peers = [dom_peer(i) for i in range(1, domains)] + [band_peer(i) for i in range(1, bands)]
    barrier = pltpu.get_barrier_semaphore()
    for peer in peers:
        pl.semaphore_signal(barrier, inc=1, device_id=peer, device_id_type=MESH)
    pl.semaphore_wait(barrier, len(peers))

    def span(index):
        return pl.ds(pl.multiple_of(index * rows, 8), rows)

    def states_of(index):
        return pl.ds(pl.multiple_of(index * state_rows, state_rows), state_rows)

    def nodes_of(index):
        return pl.ds(pl.multiple_of(index * piece, 128), piece)

    regroup = []
    for i in range(1, bands):
        peer = band_peer(i)
        regroup.append(pltpu.make_async_remote_copy(
            src_ref=filtered_ref.at[:, nodes_of(peer[1])], dst_ref=shard.at[states_of(band)],
            send_sem=send_in.at[i], recv_sem=recv_in.at[i],
            device_id=peer, device_id_type=MESH))
    for copy in regroup:
        copy.start()
    shard[states_of(band), :] = filtered_ref[:, nodes_of(band)]
    part[...] = jnp.zeros_like(part)
    for copy in regroup:
        copy.wait()

    def add_gram(i, carry):
        columns = pl.ds(pl.multiple_of(i * PIECE, PIECE), PIECE)
        value = shard[:, columns]
        part[...] += lax.dot_general(
            value * weight_ref[:, columns], value, (((1,), (1,)), ((), ())),
            preferred_element_type=jnp.float32)
        return carry

    lax.fori_loop(0, piece // PIECE, add_gram, 0)

    scatter = []
    for i in range(1, domains):
        peer = dom_peer(i)
        scatter.append(pltpu.make_async_remote_copy(
            src_ref=part.at[span(peer[0])], dst_ref=from_dom.at[i],
            send_sem=send_dom.at[i], recv_sem=recv_dom.at[i],
            device_id=peer, device_id_type=MESH))
    for copy in scatter:
        copy.start()
    own = part[span(dom), :]
    for copy in scatter:
        copy.wait()
    for i in range(1, domains):
        own = own + from_dom[i]
    from_band[band] = own
    across = []
    for i in range(1, bands):
        across.append(pltpu.make_async_remote_copy(
            src_ref=from_band.at[band], dst_ref=from_band.at[band],
            send_sem=send_band.at[i], recv_sem=recv_band.at[i],
            device_id=band_peer(i), device_id_type=MESH))
    for copy in across:
        copy.start()
    for copy in across:
        copy.wait()
    summed = from_band[0]
    for i in range(1, bands):
        summed = summed + from_band[i]
    total[span(dom), :] = summed
    back = []
    for i in range(1, domains):
        back.append(pltpu.make_async_remote_copy(
            src_ref=total.at[span(dom)], dst_ref=total.at[span(dom)],
            send_sem=send_back.at[i], recv_sem=recv_back.at[i],
            device_id=dom_peer(i), device_id_type=MESH))
    for copy in back:
        copy.start()
    for copy in back:
        copy.wait()
    mixing[...] = newton(total[...]).T.astype(jnp.bfloat16)

    def rotate(i, carry):
        columns = pl.ds(pl.multiple_of(i * PIECE, PIECE), PIECE)
        turned[:, columns] = jnp.dot(
            mixing[...], shard[:, columns], preferred_element_type=jnp.float32
        ).astype(jnp.bfloat16)
        return carry

    lax.fori_loop(0, piece // PIECE, rotate, 0)
    give = []
    for i in range(1, bands):
        peer = band_peer(i)
        give.append(pltpu.make_async_remote_copy(
            src_ref=turned.at[states_of(peer[1])], dst_ref=out_ref.at[:, nodes_of(band)],
            send_sem=send_out.at[i], recv_sem=recv_out.at[i],
            device_id=peer, device_id_type=MESH))
    for copy in give:
        copy.start()
    out_ref[:, nodes_of(band)] = turned[states_of(band), :]
    for copy in give:
        copy.wait()


PIECE = 512


def closing(filtered, weight):
    domains, bands = lax.axis_size("dom"), lax.axis_size("band")
    state_rows, nodes = filtered.shape
    size = bands * state_rows
    piece = nodes // bands
    rows = size // domains
    return pl.pallas_call(
        functools.partial(closing_kernel, domains, bands),
        in_specs=[vmem()] * 2,
        out_specs=vmem(),
        out_shape=jax.ShapeDtypeStruct(filtered.shape, jnp.bfloat16),
        scratch_shapes=[
            pltpu.VMEM((size, piece), jnp.bfloat16),
            pltpu.VMEM((size, piece), jnp.bfloat16),
            pltpu.VMEM((size, size), jnp.bfloat16),
            pltpu.VMEM((size, size), jnp.float32),
            pltpu.VMEM((domains, rows, size), jnp.float32),
            pltpu.VMEM((bands, rows, size), jnp.float32),
            pltpu.VMEM((size, size), jnp.float32),
        ] + [pltpu.SemaphoreType.DMA((bands,))] * 4
        + [pltpu.SemaphoreType.DMA((domains,))] * 2
        + [pltpu.SemaphoreType.DMA((bands,))] * 2
        + [pltpu.SemaphoreType.DMA((domains,))] * 2,
        compiler_params=pltpu.CompilerParams(
            vmem_limit_bytes=VMEM_LIMIT, collective_id=0, has_side_effects=True
        ),
        name="closing",
    )(filtered, weight)


def body(states, cell_kinetic, cell_scale, cell_potential, connectivity, shared_nodes, cell_counts):
    domain = lax.axis_index("dom")
    domains = lax.axis_size("dom")
    state_rows, node_total = states.shape
    cells, width = connectivity.shape
    faces = shared_nodes[0]
    shared = faces.shape[1]
    tail = width // 4
    half = node_total // 2
    lanes = 2 * state_rows
    ops, diag = operators(
        connectivity, cell_kinetic, cell_potential, cell_counts, node_total, state_rows
    )
    sides = jnp.stack([domain > 0, domain < domains - 1]).astype(jnp.int32)
    face_nodes = faces.reshape(2 * shared, 1)
    spots = jnp.where(faces >= half, faces - half, faces)

    field_shape = jax.ShapeDtypeStruct((half, lanes), jnp.bfloat16)
    outs = [
        jax.ShapeDtypeStruct((half, lanes), jnp.float32),
        jax.ShapeDtypeStruct((shared // 2, lanes), jnp.bfloat16),
        jax.ShapeDtypeStruct((shared // 2, lanes), jnp.bfloat16),
        field_shape,
    ]
    scratch = [
        pltpu.VMEM((half + tail, lanes), jnp.bfloat16),
        pltpu.VMEM((half + tail, lanes), jnp.float32),
        pltpu.VMEM((2 * shared, lanes), jnp.float32),
    ]
    total_scratch = [
        pltpu.VMEM((node_total, state_rows), jnp.float32),
        pltpu.VMEM((2 * shared, state_rows), jnp.float32),
    ]
    group = GROUP // 2
    steps = cells // GROUP
    ops_specs = [
        pl.BlockSpec((group, width, width), lambda g: (g, 0, 0)),
        pl.BlockSpec((group, width, width), lambda g: (g + steps, 0, 0)),
    ]
    local, left, right, previous = pl.pallas_call(
        first_kernel,
        grid=(steps,),
        in_specs=[smem()] * 3 + [vmem()] + ops_specs + [vmem()] * 2,
        out_specs=[vmem()] * 4,
        out_shape=outs,
        scratch_shapes=scratch,
        compiler_params=params(),
        name="apply_first",
    )(cell_counts, cell_scale, spots, face_nodes, ops, ops, diag, states)
    current = previous
    for k in range(1, CHEB):
        halo = exchange(left, right)
        local, left, right, field = pl.pallas_call(
            functools.partial(next_kernel, k > 1),
            grid=(steps,),
            in_specs=[smem()] * 5 + [vmem()] + ops_specs + [vmem()] * 5,
            out_specs=[vmem()] * 4,
            out_shape=outs,
            scratch_shapes=scratch + total_scratch,
            compiler_params=params(),
            name="apply_next",
        )(
            cell_counts, cell_scale, faces, spots, sides, face_nodes, ops, ops, diag, previous,
            local, *halo
        )
        previous = current
        current = field
    halo = exchange(left, right)
    filtered = pl.pallas_call(
        last_kernel,
        in_specs=[smem()] * 2 + [vmem()] * 4,
        out_specs=vmem(),
        out_shape=jax.ShapeDtypeStruct((state_rows, node_total), jnp.bfloat16),
        scratch_shapes=total_scratch,
        compiler_params=params(),
        name="finish",
    )(faces, sides, previous, local, *halo)

    piece_nodes = node_total // lax.axis_size("band")
    nodes = lax.axis_index("band") * piece_nodes + jnp.arange(piece_nodes, dtype=jnp.int32)
    has_left = (domain > 0).astype(jnp.float32)
    has_right = (domain < domains - 1).astype(jnp.float32)
    on_left = jnp.sum((nodes[None, :] == faces[0][:, None]).astype(jnp.float32), axis=0)
    on_right = jnp.sum((nodes[None, :] == faces[1][:, None]).astype(jnp.float32), axis=0)
    weight = (1.0 / (1.0 + has_left * on_left + has_right * on_right)).astype(jnp.bfloat16)
    return closing(filtered, weight[None])


def solution(mesh):
    in_specs = (
        P("band", "dom"),
        P(),
        P("dom"),
        P("dom", None),
        P("dom", None),
        P("dom", None, None),
        P("dom"),
    )
    out_specs = P("band", "dom")
    return jax.shard_map(body, mesh=mesh, in_specs=in_specs, out_specs=out_specs, check_vma=False)
```

```python
import functools

import jax
import jax.numpy as jnp
from jax import lax
from jax.experimental import pallas as pl
from jax.experimental.pallas import tpu as pltpu
from jax.sharding import PartitionSpec as P

CHEB = 4
NS_ITERS = 5
GROUP = 4
VMEM_LIMIT = 56 * 1024 * 1024
MESH = pl.DeviceIdType.MESH


def params():
    return pltpu.CompilerParams(vmem_limit_bytes=VMEM_LIMIT)


def vmem():
    return pl.BlockSpec(memory_space=pltpu.VMEM)


def smem():
    return pl.BlockSpec(memory_space=pltpu.SMEM)


def operators_kernel(node_total, counts_ref, conn_ref, pot_ref, kinetic_ref, ops_ref, diag_ref, ext):
    group, width, _ = ops_ref.shape
    step = 3 * width // 4
    first = pl.program_id(0) * group

    @pl.when(pl.program_id(0) == 0)
    def _():
        ext[...] = jnp.zeros_like(ext)

    for j in range(group):
        cell = first + j
        slots = conn_ref[pl.ds(cell, 1), :] - cell * step
        slots = jnp.where(slots < 0, slots + node_total, slots)
        hit = lax.broadcasted_iota(jnp.int32, (width, width), 0) == slots
        perm = jnp.where(hit, 1.0, 0.0).astype(jnp.bfloat16)
        rows = jnp.dot(perm, kinetic_ref[...], preferred_element_type=jnp.float32)
        ops_ref[j] = lax.dot_general(
            rows.astype(jnp.bfloat16), perm, (((1,), (1,)), ((), ())),
            preferred_element_type=jnp.float32,
        ).astype(jnp.bfloat16)
        alive = jnp.where(cell < counts_ref[0], 1.0, 0.0)
        column = jnp.sum(jnp.where(hit, pot_ref[pl.ds(cell, 1), :] * alive, 0.0), axis=1, keepdims=True)
        span = pl.ds(pl.multiple_of(cell * step, 128), width)
        ext[span, :] = ext[span, :] + column

    @pl.when(pl.program_id(0) == pl.num_programs(0) - 1)
    def _():
        tail = width - step
        half, lanes = diag_ref.shape
        ext[:tail] = ext[:tail] + ext[node_total:]
        low = lax.broadcasted_iota(jnp.int32, (ROWS, lanes), 1) < lanes // 2
        for i in range(half // ROWS):
            diag_ref[i * ROWS : (i + 1) * ROWS] = jnp.where(
                low, ext[i * ROWS : (i + 1) * ROWS], ext[half + i * ROWS : half + (i + 1) * ROWS]
            )


def operators(connectivity, cell_kinetic, cell_potential, cell_counts, node_total, state_rows):
    cells, width = connectivity.shape
    tail = width // 4
    blocks = cells // 2 // GROUP
    return pl.pallas_call(
        functools.partial(operators_kernel, node_total),
        grid=(cells // GROUP,),
        in_specs=[
            smem(),
            pl.BlockSpec((cells, width), lambda g: (0, 0)),
            pl.BlockSpec((cells, width), lambda g: (0, 0)),
            pl.BlockSpec((width, width), lambda g: (0, 0)),
        ],
        out_specs=[
            pl.BlockSpec((GROUP, width, width), lambda g: (g % blocks, g // blocks, 0)),
            pl.BlockSpec((node_total // 2, 2 * state_rows), lambda g: (0, 0)),
        ],
        out_shape=[
            jax.ShapeDtypeStruct((cells // 2, 2 * width, width), jnp.bfloat16),
            jax.ShapeDtypeStruct((node_total // 2, 2 * state_rows), jnp.float32),
        ],
        scratch_shapes=[pltpu.VMEM((node_total + tail, 1), jnp.float32)],
        compiler_params=params(),
        name="window_operators",
    )(cell_counts, connectivity, cell_potential, cell_kinetic)


CHUNK = 64


ROWS = 768


def by_rows(total, visit):
    def step(i, carry):
        visit(pl.multiple_of(i * ROWS, ROWS))
        return carry

    lax.fori_loop(0, total // ROWS, step, 0)


def swap_halves(value):
    lanes = value.shape[1]
    return jnp.concatenate([value[:, lanes // 2 :], value[:, : lanes // 2]], axis=1)


def add_faces(sides_ref, faces_ref, own_ref, from_refs, halo, total):
    shared = faces_ref.shape[1]
    for side, packed in enumerate(from_refs):
        half, lanes = packed.shape
        base = side * shared
        rows = jnp.where(sides_ref[side] > 0, packed[...].astype(jnp.float32), 0.0)
        rows = rows + own_ref[side * half : (side + 1) * half]
        halo[base : base + half] = rows[:, : lanes // 2]
        halo[base + half : base + shared] = rows[:, lanes // 2 :]
    for side in range(2):

        def visit(i, carry, side=side):
            base = i * CHUNK
            block = halo.at[pl.ds(pl.multiple_of(side * shared + base, CHUNK), CHUNK)]
            for j in range(CHUNK):
                total[pl.ds(faces_ref[side, base + j], 1), :] = block[j : j + 1, :]
            return carry

        lax.fori_loop(0, shared // CHUNK, visit, 0)


def pick_faces(faces_ref, total, halo, own_ref, to_refs):
    shared = faces_ref.shape[1]
    half = shared // 2
    for side in range(2):

        def visit(i, carry, side=side):
            base = i * CHUNK
            block = halo.at[pl.ds(pl.multiple_of(side * shared + base, CHUNK), CHUNK)]
            for j in range(CHUNK):
                block[j : j + 1, :] = total[pl.ds(faces_ref[side, base + j], 1), :]
            return carry

        lax.fori_loop(0, shared // CHUNK, visit, 0)
        base = side * shared
        rows = jnp.concatenate([halo[base : base + half], halo[base + half : base + shared]], axis=1)
        own_ref[side * half : (side + 1) * half] = rows
        to_refs[side][...] = rows.astype(to_refs[side].dtype)


def apply_cells(counts_ref, scale_ref, ops_ref, field, ext):
    group, _, width = ops_ref.shape
    step = 3 * width // 4
    lanes = ext.shape[1]
    low = lax.broadcasted_iota(jnp.int32, (1, lanes), 1) < lanes // 2
    for j in range(group):
        cell = pl.program_id(0) * group + j
        upper = cell + pl.num_programs(0) * group
        span = pl.ds(pl.multiple_of(cell * step, 128), width)
        scale = jnp.where(cell < counts_ref[0], scale_ref[cell], 0.0)
        upper_scale = jnp.where(upper < counts_ref[0], scale_ref[upper], 0.0)
        window = field[span, :]
        both = jnp.dot(ops_ref[j], window, preferred_element_type=jnp.float32)
        ext[span, :] = ext[span, :] + jnp.where(
            low, both[:width] * scale, both[width:] * upper_scale
        )


def finish_cells(faces_ref, local_ref, left_ref, right_ref, own_ref, ext, total, halo):
    half, lanes = local_ref.shape
    tail = ext.shape[0] - half
    ext[:tail] = ext[:tail] + swap_halves(ext[half:])

    def emit(base):
        value = ext[pl.ds(base, ROWS), :]
        local_ref[pl.ds(base, ROWS), :] = value
        total[pl.ds(base, ROWS), :] = value[:, : lanes // 2]
        total[pl.ds(half + base, ROWS), :] = value[:, lanes // 2 :]

    by_rows(half, emit)
    pick_faces(faces_ref, total, halo, own_ref, (left_ref, right_ref))


def start_tail(field, ext, half):
    tail = ext.shape[0] - half
    field[half:] = swap_halves(field[:tail])
    ext[half:] = jnp.zeros((tail, ext.shape[1]), jnp.float32)


def first_kernel(counts_ref, scale_ref, faces_ref, ops_ref, diag_ref, states_ref,
                 local_ref, left_ref, right_ref, own_ref, field_ref, field, ext, total, halo):
    half = local_ref.shape[0]

    @pl.when(pl.program_id(0) == 0)
    def _():
        def load(i, carry):
            low = pl.ds(pl.multiple_of(i * 128, 128), 128)
            high = pl.ds(pl.multiple_of(half + i * 128, 128), 128)
            pair = jnp.concatenate([states_ref[:, low], states_ref[:, high]], axis=0)
            value = pair.astype(jnp.float32).T
            rounded = value.astype(jnp.bfloat16)
            field[low, :] = rounded
            field_ref[low, :] = rounded
            ext[low, :] = value * diag_ref[low, :]
            return carry

        lax.fori_loop(0, half // 128, load, 0, unroll=6)
        start_tail(field, ext, half)

    apply_cells(counts_ref, scale_ref, ops_ref, field, ext)

    @pl.when(pl.program_id(0) == pl.num_programs(0) - 1)
    def _():
        finish_cells(faces_ref, local_ref, left_ref, right_ref, own_ref, ext, total, halo)


def unpack_local(old_ref, total):
    half, lanes = old_ref.shape

    def load(base):
        value = old_ref[pl.ds(base, ROWS), :]
        total[pl.ds(base, ROWS), :] = value[:, : lanes // 2]
        total[pl.ds(half + base, ROWS), :] = value[:, lanes // 2 :]

    by_rows(half, load)


def next_kernel(twice, counts_ref, scale_ref, faces_ref, sides_ref, ops_ref,
                diag_ref, prev_ref, old_ref, old_own, from_left, from_right,
                local_ref, left_ref, right_ref, own_ref, field_ref, field, ext, total, halo):
    half = local_ref.shape[0]

    @pl.when(pl.program_id(0) == 0)
    def _():
        unpack_local(old_ref, total)
        add_faces(sides_ref, faces_ref, old_own, (from_left, from_right), halo, total)

        def combine(base):
            rows = pl.ds(base, ROWS)
            value = jnp.concatenate([total[rows, :], total[pl.ds(half + base, ROWS), :]], axis=1)
            if twice:
                value = 2.0 * value - prev_ref[rows, :].astype(jnp.float32)
            value = value.astype(jnp.bfloat16)
            field[rows, :] = value
            field_ref[rows, :] = value
            ext[rows, :] = value.astype(jnp.float32) * diag_ref[rows, :]

        by_rows(half, combine)
        start_tail(field, ext, half)

    apply_cells(counts_ref, scale_ref, ops_ref, field, ext)

    @pl.when(pl.program_id(0) == pl.num_programs(0) - 1)
    def _():
        finish_cells(faces_ref, local_ref, left_ref, right_ref, own_ref, ext, total, halo)


def last_kernel(faces_ref, sides_ref, prev_ref, old_ref, old_own, from_left, from_right, field_ref,
                total, halo):
    half, lanes = old_ref.shape
    unpack_local(old_ref, total)
    add_faces(sides_ref, faces_ref, old_own, (from_left, from_right), halo, total)

    def combine(i, carry):
        low = pl.ds(pl.multiple_of(i * 128, 128), 128)
        high = pl.ds(pl.multiple_of(half + i * 128, 128), 128)
        value = jnp.concatenate([total[low, :], total[high, :]], axis=1)
        value = (2.0 * value - prev_ref[low, :].astype(jnp.float32)).T
        field_ref[:, low] = value[: lanes // 2].astype(jnp.bfloat16)
        field_ref[:, high] = value[lanes // 2 :].astype(jnp.bfloat16)
        return carry

    lax.fori_loop(0, half // 128, combine, 0, unroll=6)


def exchange_kernel(domains, left_ref, right_ref, from_left, from_right,
                    send_up, send_down, recv_up, recv_down):
    dom, band = lax.axis_index("dom"), lax.axis_index("band")
    barrier = pltpu.get_barrier_semaphore()
    has_left, has_right = dom > 0, dom < domains - 1

    @pl.when(has_left)
    def _():
        pl.semaphore_signal(barrier, inc=1, device_id=(dom - 1, band), device_id_type=MESH)

    @pl.when(has_right)
    def _():
        pl.semaphore_signal(barrier, inc=1, device_id=(dom + 1, band), device_id_type=MESH)

    pl.semaphore_wait(barrier, jnp.where(has_left & has_right, 2, 1))

    down = pltpu.make_async_remote_copy(
        src_ref=left_ref, dst_ref=from_right, send_sem=send_down, recv_sem=recv_down,
        device_id=(dom - 1, band), device_id_type=MESH)
    up = pltpu.make_async_remote_copy(
        src_ref=right_ref, dst_ref=from_left, send_sem=send_up, recv_sem=recv_up,
        device_id=(dom + 1, band), device_id_type=MESH)

    @pl.when(has_left)
    def _():
        down.start()

    @pl.when(has_right)
    def _():
        up.start()

    @pl.when(has_left)
    def _():
        down.wait_send()
        up.wait_recv()

    @pl.when(has_right)
    def _():
        up.wait_send()
        down.wait_recv()


def exchange(left, right):
    anywhere = pl.BlockSpec(memory_space=pl.ANY)
    return pl.pallas_call(
        functools.partial(exchange_kernel, lax.axis_size("dom")),
        in_specs=[anywhere] * 2,
        out_specs=[anywhere] * 2,
        out_shape=[jax.ShapeDtypeStruct(left.shape, left.dtype)] * 2,
        scratch_shapes=[pltpu.SemaphoreType.DMA] * 4,
        compiler_params=pltpu.CompilerParams(collective_id=1, has_side_effects=True),
        name="exchange",
    )(left, right)


def newton(gram_matrix):
    size = gram_matrix.shape[0]
    identity = (
        lax.broadcasted_iota(jnp.int32, (size, size), 0)
        == lax.broadcasted_iota(jnp.int32, (size, size), 1)
    ).astype(jnp.float32)
    frobenius = jnp.sqrt(jnp.sum(gram_matrix * gram_matrix))
    scaled = gram_matrix / frobenius
    inverse_root = None
    for repeat in range(NS_ITERS):
        if repeat == 0:
            factor = 1.5 * identity - 0.5 * scaled
            inverse_root = factor
        else:
            factor = 1.5 * identity - 0.5 * jnp.dot(
                inverse_root, scaled, precision=lax.Precision.HIGHEST
            )
            inverse_root = jnp.dot(factor, inverse_root, precision=lax.Precision.HIGHEST)
        if repeat < NS_ITERS - 1:
            scaled = jnp.dot(scaled, factor, precision=lax.Precision.HIGHEST)
    return inverse_root


def closing_kernel(domains, bands, filtered_ref, faces_ref, out_ref, shard, turned, mixing, part, weight,
                   from_dom, from_band, total,
                   send_in, recv_in, send_out, recv_out,
                   send_dom, recv_dom, send_band, recv_band, send_back, recv_back):
    dom, band = lax.axis_index("dom"), lax.axis_index("band")
    rows = part.shape[0] // domains
    state_rows = filtered_ref.shape[0]
    piece = shard.shape[1]

    def dom_peer(i):
        return (lax.rem(dom + i, domains), band)

    def band_peer(i):
        return (dom, lax.rem(band + i, bands))

    peers = [dom_peer(i) for i in range(1, domains)] + [band_peer(i) for i in range(1, bands)]
    barrier = pltpu.get_barrier_semaphore()
    for peer in peers:
        pl.semaphore_signal(barrier, inc=1, device_id=peer, device_id_type=MESH)
    pl.semaphore_wait(barrier, len(peers))

    def span(index):
        return pl.ds(pl.multiple_of(index * rows, 8), rows)

    def states_of(index):
        return pl.ds(pl.multiple_of(index * state_rows, state_rows), state_rows)

    def nodes_of(index):
        return pl.ds(pl.multiple_of(index * piece, 128), piece)

    regroup = []
    for i in range(1, bands):
        peer = band_peer(i)
        regroup.append(pltpu.make_async_remote_copy(
            src_ref=filtered_ref.at[:, nodes_of(peer[1])], dst_ref=shard.at[states_of(band)],
            send_sem=send_in.at[i], recv_sem=recv_in.at[i],
            device_id=peer, device_id_type=MESH))
    for copy in regroup:
        copy.start()
    shard[states_of(band), :] = filtered_ref[:, nodes_of(band)]
    part[...] = jnp.zeros_like(part)
    has_left = jnp.where(dom > 0, 1.0, 0.0)
    has_right = jnp.where(dom < domains - 1, 1.0, 0.0)

    def weigh(i, carry):
        shape = (128, faces_ref.shape[1])
        nodes = band * piece + i * 128 + lax.broadcasted_iota(jnp.int32, shape, 0)
        uses = jnp.where(faces_ref[0:1, :] == nodes, has_left, 0.0)
        uses = uses + jnp.where(faces_ref[1:2, :] == nodes, has_right, 0.0)
        column = 1.0 / (1.0 + jnp.sum(uses, axis=1, keepdims=True))
        row = jnp.broadcast_to(column, (128, 128)).T[:8]
        weight[:, pl.ds(pl.multiple_of(i * 128, 128), 128)] = row
        return carry

    lax.fori_loop(0, piece // 128, weigh, 0)
    for copy in regroup:
        copy.wait()

    def add_gram(i, carry):
        columns = pl.ds(pl.multiple_of(i * PIECE, PIECE), PIECE)
        value = shard[:, columns]
        part[...] += lax.dot_general(
            value * weight[0:1, columns].astype(jnp.bfloat16), value, (((1,), (1,)), ((), ())),
            preferred_element_type=jnp.float32)
        return carry

    lax.fori_loop(0, piece // PIECE, add_gram, 0)

    scatter = []
    for i in range(1, domains):
        peer = dom_peer(i)
        scatter.append(pltpu.make_async_remote_copy(
            src_ref=part.at[span(peer[0])], dst_ref=from_dom.at[i],
            send_sem=send_dom.at[i], recv_sem=recv_dom.at[i],
            device_id=peer, device_id_type=MESH))
    for copy in scatter:
        copy.start()
    own = part[span(dom), :]
    for copy in scatter:
        copy.wait()
    for i in range(1, domains):
        own = own + from_dom[i]
    from_band[band] = own
    across = []
    for i in range(1, bands):
        across.append(pltpu.make_async_remote_copy(
            src_ref=from_band.at[band], dst_ref=from_band.at[band],
            send_sem=send_band.at[i], recv_sem=recv_band.at[i],
            device_id=band_peer(i), device_id_type=MESH))
    for copy in across:
        copy.start()
    for copy in across:
        copy.wait()
    summed = from_band[0]
    for i in range(1, bands):
        summed = summed + from_band[i]
    total[span(dom), :] = summed
    back = []
    for i in range(1, domains):
        back.append(pltpu.make_async_remote_copy(
            src_ref=total.at[span(dom)], dst_ref=total.at[span(dom)],
            send_sem=send_back.at[i], recv_sem=recv_back.at[i],
            device_id=dom_peer(i), device_id_type=MESH))
    for copy in back:
        copy.start()
    for copy in back:
        copy.wait()
    mixing[...] = newton(total[...]).T.astype(jnp.bfloat16)

    def rotate(i, carry):
        columns = pl.ds(pl.multiple_of(i * PIECE, PIECE), PIECE)
        turned[:, columns] = jnp.dot(
            mixing[...], shard[:, columns], preferred_element_type=jnp.float32
        ).astype(jnp.bfloat16)
        return carry

    lax.fori_loop(0, piece // PIECE, rotate, 0)
    give = []
    for i in range(1, bands):
        peer = band_peer(i)
        give.append(pltpu.make_async_remote_copy(
            src_ref=turned.at[states_of(peer[1])], dst_ref=out_ref.at[:, nodes_of(band)],
            send_sem=send_out.at[i], recv_sem=recv_out.at[i],
            device_id=peer, device_id_type=MESH))
    for copy in give:
        copy.start()
    out_ref[:, nodes_of(band)] = turned[states_of(band), :]
    for copy in give:
        copy.wait()


PIECE = 512


def closing(filtered, faces):
    domains, bands = lax.axis_size("dom"), lax.axis_size("band")
    state_rows, nodes = filtered.shape
    size = bands * state_rows
    piece = nodes // bands
    rows = size // domains
    return pl.pallas_call(
        functools.partial(closing_kernel, domains, bands),
        in_specs=[vmem()] * 2,
        out_specs=vmem(),
        out_shape=jax.ShapeDtypeStruct(filtered.shape, jnp.bfloat16),
        scratch_shapes=[
            pltpu.VMEM((size, piece), jnp.bfloat16),
            pltpu.VMEM((size, piece), jnp.bfloat16),
            pltpu.VMEM((size, size), jnp.bfloat16),
            pltpu.VMEM((size, size), jnp.float32),
            pltpu.VMEM((8, piece), jnp.float32),
            pltpu.VMEM((domains, rows, size), jnp.float32),
            pltpu.VMEM((bands, rows, size), jnp.float32),
            pltpu.VMEM((size, size), jnp.float32),
        ] + [pltpu.SemaphoreType.DMA((bands,))] * 4
        + [pltpu.SemaphoreType.DMA((domains,))] * 2
        + [pltpu.SemaphoreType.DMA((bands,))] * 2
        + [pltpu.SemaphoreType.DMA((domains,))] * 2,
        compiler_params=pltpu.CompilerParams(
            vmem_limit_bytes=VMEM_LIMIT, collective_id=0, has_side_effects=True
        ),
        name="closing",
    )(filtered, faces)


def body(states, cell_kinetic, cell_scale, cell_potential, connectivity, shared_nodes, cell_counts):
    domain = lax.axis_index("dom")
    domains = lax.axis_size("dom")
    state_rows, node_total = states.shape
    cells, width = connectivity.shape
    faces = shared_nodes[0]
    shared = faces.shape[1]
    tail = width // 4
    half = node_total // 2
    lanes = 2 * state_rows
    ops, diag = operators(
        connectivity, cell_kinetic, cell_potential, cell_counts, node_total, state_rows
    )
    sides = jnp.stack([domain > 0, domain < domains - 1]).astype(jnp.int32)

    field_shape = jax.ShapeDtypeStruct((half, lanes), jnp.bfloat16)
    outs = [
        jax.ShapeDtypeStruct((half, lanes), jnp.float32),
        jax.ShapeDtypeStruct((shared // 2, lanes), jnp.bfloat16),
        jax.ShapeDtypeStruct((shared // 2, lanes), jnp.bfloat16),
        jax.ShapeDtypeStruct((shared, lanes), jnp.float32),
        field_shape,
    ]
    total_scratch = [
        pltpu.VMEM((node_total, state_rows), jnp.float32),
        pltpu.VMEM((2 * shared, state_rows), jnp.float32),
    ]
    scratch = [
        pltpu.VMEM((half + tail, lanes), jnp.bfloat16),
        pltpu.VMEM((half + tail, lanes), jnp.float32),
    ] + total_scratch
    group = GROUP // 2
    steps = cells // GROUP
    ops_spec = pl.BlockSpec((group, 2 * width, width), lambda g: (g, 0, 0))
    local, left, right, own, previous = pl.pallas_call(
        first_kernel,
        grid=(steps,),
        in_specs=[smem()] * 3 + [ops_spec] + [vmem()] * 2,
        out_specs=[vmem()] * 5,
        out_shape=outs,
        scratch_shapes=scratch,
        compiler_params=params(),
        name="apply_first",
    )(cell_counts, cell_scale, faces, ops, diag, states)
    current = previous
    for k in range(1, CHEB):
        halo = exchange(left, right)
        local, left, right, own, field = pl.pallas_call(
            functools.partial(next_kernel, k > 1),
            grid=(steps,),
            in_specs=[smem()] * 4 + [ops_spec] + [vmem()] * 6,
            out_specs=[vmem()] * 5,
            out_shape=outs,
            scratch_shapes=scratch,
            compiler_params=params(),
            name="apply_next",
        )(cell_counts, cell_scale, faces, sides, ops, diag, previous, local, own, *halo)
        previous = current
        current = field
    halo = exchange(left, right)
    filtered = pl.pallas_call(
        last_kernel,
        in_specs=[smem()] * 2 + [vmem()] * 5,
        out_specs=vmem(),
        out_shape=jax.ShapeDtypeStruct((state_rows, node_total), jnp.bfloat16),
        scratch_shapes=total_scratch,
        compiler_params=params(),
        name="finish",
    )(faces, sides, previous, local, own, *halo)
    return closing(filtered, faces)


def solution(mesh):
    in_specs = (
        P("band", "dom"),
        P(),
        P("dom"),
        P("dom", None),
        P("dom", None),
        P("dom", None, None),
        P("dom"),
    )
    out_specs = P("band", "dom")
    return jax.shard_map(body, mesh=mesh, in_specs=in_specs, out_specs=out_specs, check_vma=False)
```

```python
import functools

import jax
import jax.numpy as jnp
from jax import lax
from jax.experimental import pallas as pl
from jax.experimental.pallas import tpu as pltpu
from jax.sharding import PartitionSpec as P

CHEB = 4
NS_ITERS = 5
GROUP = 4
MESH = pl.DeviceIdType.MESH


def params(mib=56):
    return pltpu.CompilerParams(vmem_limit_bytes=mib * 1024 * 1024)


def vmem():
    return pl.BlockSpec(memory_space=pltpu.VMEM)


def smem():
    return pl.BlockSpec(memory_space=pltpu.SMEM)


def operators_kernel(counts_ref, scale_ref, faces_ref, conn_ref, pot_ref, kinetic_ref, states_ref,
                     ops_ref, diag_ref, local_ref, left_ref, right_ref, own_ref, field_ref,
                     column_sum, field, ext, total, halo):
    group, width, _ = ops_ref.shape
    step = 3 * width // 4
    half, lanes = local_ref.shape
    node_total = 2 * half
    first = pl.program_id(0) * group
    pairs = pl.num_programs(0) * group // 2

    @pl.when(pl.program_id(0) == 0)
    def _():
        column_sum[...] = jnp.zeros_like(column_sum)

        def load(i, carry):
            low = pl.ds(pl.multiple_of(i * 128, 128), 128)
            high = pl.ds(pl.multiple_of(half + i * 128, 128), 128)
            pair = jnp.concatenate([states_ref[:, low], states_ref[:, high]], axis=0)
            rounded = pair.astype(jnp.float32).T.astype(jnp.bfloat16)
            field[low, :] = rounded
            field_ref[low, :] = rounded
            ext[low, :] = jnp.zeros((128, lanes), jnp.float32)
            return carry

        lax.fori_loop(0, half // 128, load, 0, unroll=6)
        start_tail(field, ext, half)

    low_lane = lax.broadcasted_iota(jnp.int32, (1, lanes), 1) < lanes // 2
    for j in range(group):
        cell = first + j
        slots = conn_ref[pl.ds(cell, 1), :] - cell * step
        slots = jnp.where(slots < 0, slots + node_total, slots)
        hit = lax.broadcasted_iota(jnp.int32, (width, width), 0) == slots
        perm = jnp.where(hit, 1.0, 0.0).astype(jnp.bfloat16)
        rows = jnp.dot(perm, kinetic_ref[...], preferred_element_type=jnp.float32)
        operator = lax.dot_general(
            rows.astype(jnp.bfloat16), perm, (((1,), (1,)), ((), ())),
            preferred_element_type=jnp.float32,
        ).astype(jnp.bfloat16)
        ops_ref[j] = operator
        alive = jnp.where(cell < counts_ref[0], 1.0, 0.0)
        column = jnp.sum(
            jnp.where(hit, pot_ref[pl.ds(cell, 1), :] * alive, 0.0), axis=1, keepdims=True
        )
        span = pl.ds(pl.multiple_of(cell * step, 128), width)
        column_sum[span, :] = column_sum[span, :] + column
        upper = cell >= pairs
        scale = alive * scale_ref[cell]
        spread = jnp.where(
            low_lane, jnp.where(upper, 0.0, scale), jnp.where(upper, scale, 0.0)
        )
        place = jnp.where(upper, cell - pairs, cell)
        packed = pl.ds(pl.multiple_of(place * step, 128), width)
        product = jnp.dot(operator, field[packed, :], preferred_element_type=jnp.float32)
        ext[packed, :] = ext[packed, :] + product * spread

    @pl.when(pl.program_id(0) == pl.num_programs(0) - 1)
    def _():
        tail = width - step
        column_sum[:tail] = column_sum[:tail] + column_sum[node_total:]

        def weigh(base):
            rows = pl.ds(base, ROWS)
            value = jnp.where(low_lane, column_sum[rows, :], column_sum[pl.ds(half + base, ROWS), :])
            diag_ref[rows, :] = value
            ext[rows, :] = ext[rows, :] + value * field[rows, :].astype(jnp.float32)

        by_rows(half, weigh)
        finish_cells(faces_ref, local_ref, left_ref, right_ref, own_ref, ext, total, halo)


CHUNK = 64


ROWS = 768


def by_rows(total, visit):
    def step(i, carry):
        visit(pl.multiple_of(i * ROWS, ROWS))
        return carry

    lax.fori_loop(0, total // ROWS, step, 0)


def swap_halves(value):
    lanes = value.shape[1]
    return jnp.concatenate([value[:, lanes // 2 :], value[:, : lanes // 2]], axis=1)


def add_faces(sides_ref, faces_ref, own_ref, from_refs, halo, total):
    shared = faces_ref.shape[1]
    for side, packed in enumerate(from_refs):
        half, lanes = packed.shape
        base = side * shared
        rows = jnp.where(sides_ref[side] > 0, packed[...].astype(jnp.float32), 0.0)
        rows = rows + own_ref[side * half : (side + 1) * half]
        halo[base : base + half] = rows[:, : lanes // 2]
        halo[base + half : base + shared] = rows[:, lanes // 2 :]
    for side in range(2):

        def visit(i, carry, side=side):
            base = i * CHUNK
            block = halo.at[pl.ds(pl.multiple_of(side * shared + base, CHUNK), CHUNK)]
            for j in range(CHUNK):
                total[pl.ds(faces_ref[side, base + j], 1), :] = block[j : j + 1, :]
            return carry

        lax.fori_loop(0, shared // CHUNK, visit, 0)


def pick_faces(faces_ref, total, halo, own_ref, to_refs):
    shared = faces_ref.shape[1]
    half = shared // 2
    for side in range(2):

        def visit(i, carry, side=side):
            base = i * CHUNK
            block = halo.at[pl.ds(pl.multiple_of(side * shared + base, CHUNK), CHUNK)]
            for j in range(CHUNK):
                block[j : j + 1, :] = total[pl.ds(faces_ref[side, base + j], 1), :]
            return carry

        lax.fori_loop(0, shared // CHUNK, visit, 0)
        base = side * shared
        rows = jnp.concatenate([halo[base : base + half], halo[base + half : base + shared]], axis=1)
        own_ref[side * half : (side + 1) * half] = rows
        to_refs[side][...] = rows.astype(to_refs[side].dtype)


def apply_cells(counts_ref, scale_ref, ops_ref, field, ext):
    group, _, width = ops_ref.shape
    step = 3 * width // 4
    lanes = ext.shape[1]
    low = lax.broadcasted_iota(jnp.int32, (1, lanes), 1) < lanes // 2
    for j in range(group):
        cell = pl.program_id(0) * group + j
        upper = cell + pl.num_programs(0) * group
        span = pl.ds(pl.multiple_of(cell * step, 128), width)
        scale = jnp.where(cell < counts_ref[0], scale_ref[cell], 0.0)
        upper_scale = jnp.where(upper < counts_ref[0], scale_ref[upper], 0.0)
        window = field[span, :]
        both = jnp.dot(ops_ref[j], window, preferred_element_type=jnp.float32)
        ext[span, :] = ext[span, :] + jnp.where(
            low, both[:width] * scale, both[width:] * upper_scale
        )


def finish_cells(faces_ref, local_ref, left_ref, right_ref, own_ref, ext, total, halo):
    half, lanes = local_ref.shape
    tail = ext.shape[0] - half
    ext[:tail] = ext[:tail] + swap_halves(ext[half:])

    def emit(base):
        value = ext[pl.ds(base, ROWS), :]
        local_ref[pl.ds(base, ROWS), :] = value
        total[pl.ds(base, ROWS), :] = value[:, : lanes // 2]
        total[pl.ds(half + base, ROWS), :] = value[:, lanes // 2 :]

    by_rows(half, emit)
    pick_faces(faces_ref, total, halo, own_ref, (left_ref, right_ref))


def start_tail(field, ext, half):
    tail = ext.shape[0] - half
    field[half:] = swap_halves(field[:tail])
    ext[half:] = jnp.zeros((tail, ext.shape[1]), jnp.float32)


def unpack_local(old_ref, total):
    half, lanes = old_ref.shape

    def load(base):
        value = old_ref[pl.ds(base, ROWS), :]
        total[pl.ds(base, ROWS), :] = value[:, : lanes // 2]
        total[pl.ds(half + base, ROWS), :] = value[:, lanes // 2 :]

    by_rows(half, load)


def next_kernel(twice, counts_ref, scale_ref, faces_ref, sides_ref, ops_ref,
                diag_ref, prev_ref, old_ref, old_own, from_left, from_right,
                local_ref, left_ref, right_ref, own_ref, field_ref, field, ext, total, halo):
    half = local_ref.shape[0]

    @pl.when(pl.program_id(0) == 0)
    def _():
        unpack_local(old_ref, total)
        add_faces(sides_ref, faces_ref, old_own, (from_left, from_right), halo, total)

        def combine(base):
            rows = pl.ds(base, ROWS)
            value = jnp.concatenate([total[rows, :], total[pl.ds(half + base, ROWS), :]], axis=1)
            if twice:
                value = 2.0 * value - prev_ref[rows, :].astype(jnp.float32)
            value = value.astype(jnp.bfloat16)
            field[rows, :] = value
            field_ref[rows, :] = value
            ext[rows, :] = value.astype(jnp.float32) * diag_ref[rows, :]

        by_rows(half, combine)
        start_tail(field, ext, half)

    apply_cells(counts_ref, scale_ref, ops_ref, field, ext)

    @pl.when(pl.program_id(0) == pl.num_programs(0) - 1)
    def _():
        finish_cells(faces_ref, local_ref, left_ref, right_ref, own_ref, ext, total, halo)


def last_kernel(faces_ref, sides_ref, prev_ref, old_ref, old_own, from_left, from_right, field_ref,
                total, halo):
    half, lanes = old_ref.shape
    unpack_local(old_ref, total)
    add_faces(sides_ref, faces_ref, old_own, (from_left, from_right), halo, total)

    def combine(i, carry):
        low = pl.ds(pl.multiple_of(i * 128, 128), 128)
        high = pl.ds(pl.multiple_of(half + i * 128, 128), 128)
        value = jnp.concatenate([total[low, :], total[high, :]], axis=1)
        value = (2.0 * value - prev_ref[low, :].astype(jnp.float32)).T
        field_ref[:, low] = value[: lanes // 2].astype(jnp.bfloat16)
        field_ref[:, high] = value[lanes // 2 :].astype(jnp.bfloat16)
        return carry

    lax.fori_loop(0, half // 128, combine, 0, unroll=6)


def exchange_kernel(domains, left_ref, right_ref, from_left, from_right,
                    send_up, send_down, recv_up, recv_down):
    dom, band = lax.axis_index("dom"), lax.axis_index("band")
    barrier = pltpu.get_barrier_semaphore()
    has_left, has_right = dom > 0, dom < domains - 1

    @pl.when(has_left)
    def _():
        pl.semaphore_signal(barrier, inc=1, device_id=(dom - 1, band), device_id_type=MESH)

    @pl.when(has_right)
    def _():
        pl.semaphore_signal(barrier, inc=1, device_id=(dom + 1, band), device_id_type=MESH)

    pl.semaphore_wait(barrier, jnp.where(has_left & has_right, 2, 1))

    down = pltpu.make_async_remote_copy(
        src_ref=left_ref, dst_ref=from_right, send_sem=send_down, recv_sem=recv_down,
        device_id=(dom - 1, band), device_id_type=MESH)
    up = pltpu.make_async_remote_copy(
        src_ref=right_ref, dst_ref=from_left, send_sem=send_up, recv_sem=recv_up,
        device_id=(dom + 1, band), device_id_type=MESH)

    @pl.when(has_left)
    def _():
        down.start()

    @pl.when(has_right)
    def _():
        up.start()

    @pl.when(has_left)
    def _():
        down.wait_send()
        up.wait_recv()

    @pl.when(has_right)
    def _():
        up.wait_send()
        down.wait_recv()


def exchange(left, right):
    anywhere = pl.BlockSpec(memory_space=pl.ANY)
    return pl.pallas_call(
        functools.partial(exchange_kernel, lax.axis_size("dom")),
        in_specs=[anywhere] * 2,
        out_specs=[anywhere] * 2,
        out_shape=[jax.ShapeDtypeStruct(left.shape, left.dtype)] * 2,
        scratch_shapes=[pltpu.SemaphoreType.DMA] * 4,
        compiler_params=pltpu.CompilerParams(
            vmem_limit_bytes=4 * 1024 * 1024, collective_id=1, has_side_effects=True
        ),
        name="exchange",
    )(left, right)


def newton(gram_matrix):
    size = gram_matrix.shape[0]
    identity = (
        lax.broadcasted_iota(jnp.int32, (size, size), 0)
        == lax.broadcasted_iota(jnp.int32, (size, size), 1)
    ).astype(jnp.float32)
    frobenius = jnp.sqrt(jnp.sum(gram_matrix * gram_matrix))
    scaled = gram_matrix / frobenius
    inverse_root = None
    for repeat in range(NS_ITERS):
        if repeat == 0:
            factor = 1.5 * identity - 0.5 * scaled
            inverse_root = factor
        else:
            factor = 1.5 * identity - 0.5 * jnp.dot(
                inverse_root, scaled, precision=lax.Precision.HIGHEST
            )
            inverse_root = jnp.dot(factor, inverse_root, precision=lax.Precision.HIGHEST)
        if repeat < NS_ITERS - 1:
            scaled = jnp.dot(scaled, factor, precision=lax.Precision.HIGHEST)
    return inverse_root


def closing_kernel(domains, bands, filtered_ref, faces_ref, out_ref, shard, turned, mixing, part, weight,
                   from_dom, from_band, total,
                   send_in, recv_in, send_out, recv_out,
                   send_dom, recv_dom, send_band, recv_band, send_back, recv_back):
    dom, band = lax.axis_index("dom"), lax.axis_index("band")
    rows = part.shape[0] // domains
    state_rows = filtered_ref.shape[0]
    piece = shard.shape[1]

    def dom_peer(i):
        return (lax.rem(dom + i, domains), band)

    def band_peer(i):
        return (dom, lax.rem(band + i, bands))

    peers = [dom_peer(i) for i in range(1, domains)] + [band_peer(i) for i in range(1, bands)]
    barrier = pltpu.get_barrier_semaphore()
    for peer in peers:
        pl.semaphore_signal(barrier, inc=1, device_id=peer, device_id_type=MESH)
    pl.semaphore_wait(barrier, len(peers))

    def span(index):
        return pl.ds(pl.multiple_of(index * rows, 8), rows)

    def states_of(index):
        return pl.ds(pl.multiple_of(index * state_rows, state_rows), state_rows)

    def nodes_of(index):
        return pl.ds(pl.multiple_of(index * piece, 128), piece)

    regroup = []
    for i in range(1, bands):
        peer = band_peer(i)
        regroup.append(pltpu.make_async_remote_copy(
            src_ref=filtered_ref.at[:, nodes_of(peer[1])], dst_ref=shard.at[states_of(band)],
            send_sem=send_in.at[i], recv_sem=recv_in.at[i],
            device_id=peer, device_id_type=MESH))
    for copy in regroup:
        copy.start()
    shard[states_of(band), :] = filtered_ref[:, nodes_of(band)]
    part[...] = jnp.zeros_like(part)
    has_left = jnp.where(dom > 0, 1.0, 0.0)
    has_right = jnp.where(dom < domains - 1, 1.0, 0.0)

    def weigh(i, carry):
        shape = (128, faces_ref.shape[1])
        nodes = band * piece + i * 128 + lax.broadcasted_iota(jnp.int32, shape, 0)
        uses = jnp.where(faces_ref[0:1, :] == nodes, has_left, 0.0)
        uses = uses + jnp.where(faces_ref[1:2, :] == nodes, has_right, 0.0)
        column = 1.0 / (1.0 + jnp.sum(uses, axis=1, keepdims=True))
        row = jnp.broadcast_to(column, (128, 128)).T[:8]
        weight[:, pl.ds(pl.multiple_of(i * 128, 128), 128)] = row
        return carry

    lax.fori_loop(0, piece // 128, weigh, 0)
    for copy in regroup:
        copy.wait()

    def add_gram(i, carry):
        columns = pl.ds(pl.multiple_of(i * PIECE, PIECE), PIECE)
        value = shard[:, columns]
        part[...] += lax.dot_general(
            value * weight[0:1, columns].astype(jnp.bfloat16), value, (((1,), (1,)), ((), ())),
            preferred_element_type=jnp.float32)
        return carry

    lax.fori_loop(0, piece // PIECE, add_gram, 0)

    scatter = []
    for i in range(1, domains):
        peer = dom_peer(i)
        scatter.append(pltpu.make_async_remote_copy(
            src_ref=part.at[span(peer[0])], dst_ref=from_dom.at[i],
            send_sem=send_dom.at[i], recv_sem=recv_dom.at[i],
            device_id=peer, device_id_type=MESH))
    for copy in scatter:
        copy.start()
    own = part[span(dom), :]
    for copy in scatter:
        copy.wait()
    for i in range(1, domains):
        own = own + from_dom[i]
    from_band[band] = own
    across = []
    for i in range(1, bands):
        across.append(pltpu.make_async_remote_copy(
            src_ref=from_band.at[band], dst_ref=from_band.at[band],
            send_sem=send_band.at[i], recv_sem=recv_band.at[i],
            device_id=band_peer(i), device_id_type=MESH))
    for copy in across:
        copy.start()
    for copy in across:
        copy.wait()
    summed = from_band[0]
    for i in range(1, bands):
        summed = summed + from_band[i]
    total[span(dom), :] = summed
    back = []
    for i in range(1, domains):
        back.append(pltpu.make_async_remote_copy(
            src_ref=total.at[span(dom)], dst_ref=total.at[span(dom)],
            send_sem=send_back.at[i], recv_sem=recv_back.at[i],
            device_id=dom_peer(i), device_id_type=MESH))
    for copy in back:
        copy.start()
    for copy in back:
        copy.wait()
    mixing[...] = newton(total[...]).T.astype(jnp.bfloat16)

    def rotate(i, carry):
        columns = pl.ds(pl.multiple_of(i * PIECE, PIECE), PIECE)
        turned[:, columns] = jnp.dot(
            mixing[...], shard[:, columns], preferred_element_type=jnp.float32
        ).astype(jnp.bfloat16)
        return carry

    lax.fori_loop(0, piece // PIECE, rotate, 0)
    give = []
    for i in range(1, bands):
        peer = band_peer(i)
        give.append(pltpu.make_async_remote_copy(
            src_ref=turned.at[states_of(peer[1])], dst_ref=out_ref.at[:, nodes_of(band)],
            send_sem=send_out.at[i], recv_sem=recv_out.at[i],
            device_id=peer, device_id_type=MESH))
    for copy in give:
        copy.start()
    out_ref[:, nodes_of(band)] = turned[states_of(band), :]
    for copy in give:
        copy.wait()


PIECE = 512


def closing(filtered, faces):
    domains, bands = lax.axis_size("dom"), lax.axis_size("band")
    state_rows, nodes = filtered.shape
    size = bands * state_rows
    piece = nodes // bands
    rows = size // domains
    return pl.pallas_call(
        functools.partial(closing_kernel, domains, bands),
        in_specs=[vmem()] * 2,
        out_specs=vmem(),
        out_shape=jax.ShapeDtypeStruct(filtered.shape, jnp.bfloat16),
        scratch_shapes=[
            pltpu.VMEM((size, piece), jnp.bfloat16),
            pltpu.VMEM((size, piece), jnp.bfloat16),
            pltpu.VMEM((size, size), jnp.bfloat16),
            pltpu.VMEM((size, size), jnp.float32),
            pltpu.VMEM((8, piece), jnp.float32),
            pltpu.VMEM((domains, rows, size), jnp.float32),
            pltpu.VMEM((bands, rows, size), jnp.float32),
            pltpu.VMEM((size, size), jnp.float32),
        ] + [pltpu.SemaphoreType.DMA((bands,))] * 4
        + [pltpu.SemaphoreType.DMA((domains,))] * 2
        + [pltpu.SemaphoreType.DMA((bands,))] * 2
        + [pltpu.SemaphoreType.DMA((domains,))] * 2,
        compiler_params=pltpu.CompilerParams(
            vmem_limit_bytes=24 * 1024 * 1024, collective_id=0, has_side_effects=True
        ),
        name="closing",
    )(filtered, faces)


def body(states, cell_kinetic, cell_scale, cell_potential, connectivity, shared_nodes, cell_counts):
    domain = lax.axis_index("dom")
    domains = lax.axis_size("dom")
    state_rows, node_total = states.shape
    cells, width = connectivity.shape
    faces = shared_nodes[0]
    shared = faces.shape[1]
    tail = width // 4
    half = node_total // 2
    lanes = 2 * state_rows
    sides = jnp.stack([domain > 0, domain < domains - 1]).astype(jnp.int32)

    field_shape = jax.ShapeDtypeStruct((half, lanes), jnp.bfloat16)
    outs = [
        jax.ShapeDtypeStruct((half, lanes), jnp.float32),
        jax.ShapeDtypeStruct((shared // 2, lanes), jnp.bfloat16),
        jax.ShapeDtypeStruct((shared // 2, lanes), jnp.bfloat16),
        jax.ShapeDtypeStruct((shared, lanes), jnp.float32),
        field_shape,
    ]
    total_scratch = [
        pltpu.VMEM((node_total, state_rows), jnp.float32),
        pltpu.VMEM((2 * shared, state_rows), jnp.float32),
    ]
    scratch = [
        pltpu.VMEM((half + tail, lanes), jnp.bfloat16),
        pltpu.VMEM((half + tail, lanes), jnp.float32),
    ] + total_scratch
    group = GROUP // 2
    steps = cells // GROUP
    ops_spec = pl.BlockSpec((group, 2 * width, width), lambda g: (g, 0, 0))
    blocks = cells // 2 // GROUP
    ops, diag, local, left, right, own, previous = pl.pallas_call(
        operators_kernel,
        grid=(cells // GROUP,),
        in_specs=[smem()] * 3 + [vmem()] * 4,
        out_specs=[
            pl.BlockSpec((GROUP, width, width), lambda g: (g % blocks, g // blocks, 0)),
        ] + [vmem()] * 6,
        out_shape=[
            jax.ShapeDtypeStruct((cells // 2, 2 * width, width), jnp.bfloat16),
            jax.ShapeDtypeStruct((half, lanes), jnp.float32),
        ] + outs,
        scratch_shapes=[pltpu.VMEM((node_total + tail, 1), jnp.float32)] + scratch,
        compiler_params=params(),
        name="operators_and_first_apply",
    )(cell_counts, cell_scale, faces, connectivity, cell_potential, cell_kinetic, states)
    current = previous
    for k in range(1, CHEB):
        halo = exchange(left, right)
        local, left, right, own, field = pl.pallas_call(
            functools.partial(next_kernel, k > 1),
            grid=(steps,),
            in_specs=[smem()] * 4 + [ops_spec] + [vmem()] * 6,
            out_specs=[vmem()] * 5,
            out_shape=outs,
            scratch_shapes=scratch,
            compiler_params=params(32),
            name="apply_next",
        )(cell_counts, cell_scale, faces, sides, ops, diag, previous, local, own, *halo)
        previous = current
        current = field
    halo = exchange(left, right)
    filtered = pl.pallas_call(
        last_kernel,
        in_specs=[smem()] * 2 + [vmem()] * 5,
        out_specs=vmem(),
        out_shape=jax.ShapeDtypeStruct((state_rows, node_total), jnp.bfloat16),
        scratch_shapes=total_scratch,
        compiler_params=params(24),
        name="finish",
    )(faces, sides, previous, local, own, *halo)
    return closing(filtered, faces)


def solution(mesh):
    in_specs = (
        P("band", "dom"),
        P(),
        P("dom"),
        P("dom", None),
        P("dom", None),
        P("dom", None, None),
        P("dom"),
    )
    out_specs = P("band", "dom")
    return jax.shard_map(body, mesh=mesh, in_specs=in_specs, out_specs=out_specs, check_vma=False)
```

```python
import functools

import jax
import jax.numpy as jnp
from jax import lax
from jax.experimental import pallas as pl
from jax.experimental.pallas import tpu as pltpu
from jax.sharding import PartitionSpec as P

CHEB = 4
NS_ITERS = 5
GROUP = 4
MESH = pl.DeviceIdType.MESH


def params(mib=56):
    return pltpu.CompilerParams(vmem_limit_bytes=mib * 1024 * 1024)


def vmem():
    return pl.BlockSpec(memory_space=pltpu.VMEM)


def smem():
    return pl.BlockSpec(memory_space=pltpu.SMEM)


def operators_kernel(counts_ref, scale_ref, faces_ref, conn_ref, pot_ref, kinetic_ref, states_ref,
                     ops_ref, diag_ref, local_ref, left_ref, right_ref, own_ref, field_ref,
                     column_sum, field, ext, total, halo):
    group, width, _ = ops_ref.shape
    step = 3 * width // 4
    half, lanes = local_ref.shape
    node_total = 2 * half
    first = pl.program_id(0) * group
    pairs = pl.num_programs(0) * group // 2

    @pl.when(pl.program_id(0) == 0)
    def _():
        column_sum[...] = jnp.zeros_like(column_sum)

        def load(i, carry):
            low = pl.ds(pl.multiple_of(i * 128, 128), 128)
            high = pl.ds(pl.multiple_of(half + i * 128, 128), 128)
            pair = jnp.concatenate([states_ref[:, low], states_ref[:, high]], axis=0)
            rounded = pair.astype(jnp.float32).T.astype(jnp.bfloat16)
            field[low, :] = rounded
            field_ref[low, :] = rounded
            ext[low, :] = jnp.zeros((128, lanes), jnp.float32)
            return carry

        lax.fori_loop(0, half // 128, load, 0, unroll=6)
        start_tail(field, ext, half)

    low_lane = lax.broadcasted_iota(jnp.int32, (1, lanes), 1) < lanes // 2
    for j in range(group):
        cell = first + j
        slots = conn_ref[pl.ds(cell, 1), :] - cell * step
        slots = jnp.where(slots < 0, slots + node_total, slots)
        hit = lax.broadcasted_iota(jnp.int32, (width, width), 0) == slots
        perm = jnp.where(hit, 1.0, 0.0).astype(jnp.bfloat16)
        rows = jnp.dot(perm, kinetic_ref[...], preferred_element_type=jnp.float32)
        operator = lax.dot_general(
            rows.astype(jnp.bfloat16), perm, (((1,), (1,)), ((), ())),
            preferred_element_type=jnp.float32,
        ).astype(jnp.bfloat16)
        ops_ref[j] = operator
        alive = jnp.where(cell < counts_ref[0], 1.0, 0.0)
        column = jnp.sum(
            jnp.where(hit, pot_ref[pl.ds(cell, 1), :] * alive, 0.0), axis=1, keepdims=True
        )
        span = pl.ds(pl.multiple_of(cell * step, 128), width)
        column_sum[span, :] = column_sum[span, :] + column
        upper = cell >= pairs
        scale = alive * scale_ref[cell]
        spread = jnp.where(
            low_lane, jnp.where(upper, 0.0, scale), jnp.where(upper, scale, 0.0)
        )
        place = jnp.where(upper, cell - pairs, cell)
        packed = pl.ds(pl.multiple_of(place * step, 128), width)
        product = jnp.dot(operator, field[packed, :], preferred_element_type=jnp.float32)
        ext[packed, :] = ext[packed, :] + product * spread

    @pl.when(pl.program_id(0) == pl.num_programs(0) - 1)
    def _():
        tail = width - step
        column_sum[:tail] = column_sum[:tail] + column_sum[node_total:]

        def weigh(base):
            rows = pl.ds(base, ROWS)
            value = jnp.where(low_lane, column_sum[rows, :], column_sum[pl.ds(half + base, ROWS), :])
            diag_ref[rows, :] = value
            ext[rows, :] = ext[rows, :] + value * field[rows, :].astype(jnp.float32)

        by_rows(half, weigh)
        finish_cells(faces_ref, local_ref, left_ref, right_ref, own_ref, ext, total, halo)


CHUNK = 64


ROWS = 768


def by_rows(total, visit):
    def step(i, carry):
        visit(pl.multiple_of(i * ROWS, ROWS))
        return carry

    lax.fori_loop(0, total // ROWS, step, 0)


def swap_halves(value):
    lanes = value.shape[1]
    return jnp.concatenate([value[:, lanes // 2 :], value[:, : lanes // 2]], axis=1)


def add_faces(sides_ref, faces_ref, own_ref, from_refs, halo, total):
    shared = faces_ref.shape[1]
    for side, packed in enumerate(from_refs):
        half, lanes = packed.shape
        base = side * shared
        rows = jnp.where(sides_ref[side] > 0, packed[...].astype(jnp.float32), 0.0)
        rows = rows + own_ref[side * half : (side + 1) * half]
        halo[base : base + half] = rows[:, : lanes // 2]
        halo[base + half : base + shared] = rows[:, lanes // 2 :]
    for side in range(2):

        def visit(i, carry, side=side):
            base = i * CHUNK
            block = halo.at[pl.ds(pl.multiple_of(side * shared + base, CHUNK), CHUNK)]
            for j in range(CHUNK):
                total[pl.ds(faces_ref[side, base + j], 1), :] = block[j : j + 1, :]
            return carry

        lax.fori_loop(0, shared // CHUNK, visit, 0)


def pick_faces(faces_ref, total, halo, own_ref, to_refs):
    shared = faces_ref.shape[1]
    half = shared // 2
    for side in range(2):

        def visit(i, carry, side=side):
            base = i * CHUNK
            block = halo.at[pl.ds(pl.multiple_of(side * shared + base, CHUNK), CHUNK)]
            for j in range(CHUNK):
                block[j : j + 1, :] = total[pl.ds(faces_ref[side, base + j], 1), :]
            return carry

        lax.fori_loop(0, shared // CHUNK, visit, 0)
        base = side * shared
        rows = jnp.concatenate([halo[base : base + half], halo[base + half : base + shared]], axis=1)
        own_ref[side * half : (side + 1) * half] = rows
        to_refs[side][...] = rows.astype(to_refs[side].dtype)


def apply_cells(counts_ref, scale_ref, ops_ref, field, ext):
    group, _, width = ops_ref.shape
    step = 3 * width // 4
    lanes = ext.shape[1]
    low = lax.broadcasted_iota(jnp.int32, (1, lanes), 1) < lanes // 2
    for j in range(group):
        cell = pl.program_id(0) * group + j
        upper = cell + pl.num_programs(0) * group
        span = pl.ds(pl.multiple_of(cell * step, 128), width)
        scale = jnp.where(cell < counts_ref[0], scale_ref[cell], 0.0)
        upper_scale = jnp.where(upper < counts_ref[0], scale_ref[upper], 0.0)
        window = field[span, :]
        both = jnp.dot(ops_ref[j], window, preferred_element_type=jnp.float32)
        ext[span, :] = ext[span, :] + jnp.where(
            low, both[:width] * scale, both[width:] * upper_scale
        )


def finish_cells(faces_ref, local_ref, left_ref, right_ref, own_ref, ext, total, halo):
    half, lanes = local_ref.shape
    tail = ext.shape[0] - half
    ext[:tail] = ext[:tail] + swap_halves(ext[half:])

    def emit(base):
        value = ext[pl.ds(base, ROWS), :]
        local_ref[pl.ds(base, ROWS), :] = value
        total[pl.ds(base, ROWS), :] = value[:, : lanes // 2]
        total[pl.ds(half + base, ROWS), :] = value[:, lanes // 2 :]

    by_rows(half, emit)
    pick_faces(faces_ref, total, halo, own_ref, (left_ref, right_ref))


def start_tail(field, ext, half):
    tail = ext.shape[0] - half
    field[half:] = swap_halves(field[:tail])
    ext[half:] = jnp.zeros((tail, ext.shape[1]), jnp.float32)


def unpack_local(old_ref, total):
    half, lanes = old_ref.shape

    def load(base):
        value = old_ref[pl.ds(base, ROWS), :]
        total[pl.ds(base, ROWS), :] = value[:, : lanes // 2]
        total[pl.ds(half + base, ROWS), :] = value[:, lanes // 2 :]

    by_rows(half, load)


def next_kernel(twice, counts_ref, scale_ref, faces_ref, sides_ref, ops_ref,
                diag_ref, prev_ref, old_ref, old_own, from_left, from_right,
                local_ref, left_ref, right_ref, own_ref, field_ref, field, ext, total, halo):
    half = local_ref.shape[0]

    @pl.when(pl.program_id(0) == 0)
    def _():
        unpack_local(old_ref, total)
        add_faces(sides_ref, faces_ref, old_own, (from_left, from_right), halo, total)

        def combine(base):
            rows = pl.ds(base, ROWS)
            value = jnp.concatenate([total[rows, :], total[pl.ds(half + base, ROWS), :]], axis=1)
            if twice:
                value = 2.0 * value - prev_ref[rows, :].astype(jnp.float32)
            value = value.astype(jnp.bfloat16)
            field[rows, :] = value
            field_ref[rows, :] = value
            ext[rows, :] = value.astype(jnp.float32) * diag_ref[rows, :]

        by_rows(half, combine)
        start_tail(field, ext, half)

    apply_cells(counts_ref, scale_ref, ops_ref, field, ext)

    @pl.when(pl.program_id(0) == pl.num_programs(0) - 1)
    def _():
        finish_cells(faces_ref, local_ref, left_ref, right_ref, own_ref, ext, total, halo)


def last_kernel(faces_ref, sides_ref, prev_ref, old_ref, old_own, from_left, from_right, field_ref,
                total, halo):
    half, lanes = old_ref.shape
    unpack_local(old_ref, total)
    add_faces(sides_ref, faces_ref, old_own, (from_left, from_right), halo, total)

    def combine(i, carry):
        low = pl.ds(pl.multiple_of(i * 128, 128), 128)
        high = pl.ds(pl.multiple_of(half + i * 128, 128), 128)
        value = jnp.concatenate([total[low, :], total[high, :]], axis=1)
        value = (2.0 * value - prev_ref[low, :].astype(jnp.float32)).T
        field_ref[:, low] = value[: lanes // 2].astype(jnp.bfloat16)
        field_ref[:, high] = value[lanes // 2 :].astype(jnp.bfloat16)
        return carry

    lax.fori_loop(0, half // 128, combine, 0, unroll=6)


def exchange_kernel(domains, left_ref, right_ref, from_left, from_right,
                    send_up, send_down, recv_up, recv_down):
    dom, band = lax.axis_index("dom"), lax.axis_index("band")
    barrier = pltpu.get_barrier_semaphore()
    has_left, has_right = dom > 0, dom < domains - 1

    @pl.when(has_left)
    def _():
        pl.semaphore_signal(barrier, inc=1, device_id=(dom - 1, band), device_id_type=MESH)

    @pl.when(has_right)
    def _():
        pl.semaphore_signal(barrier, inc=1, device_id=(dom + 1, band), device_id_type=MESH)

    pl.semaphore_wait(barrier, jnp.where(has_left & has_right, 2, 1))

    down = pltpu.make_async_remote_copy(
        src_ref=left_ref, dst_ref=from_right, send_sem=send_down, recv_sem=recv_down,
        device_id=(dom - 1, band), device_id_type=MESH)
    up = pltpu.make_async_remote_copy(
        src_ref=right_ref, dst_ref=from_left, send_sem=send_up, recv_sem=recv_up,
        device_id=(dom + 1, band), device_id_type=MESH)

    @pl.when(has_left)
    def _():
        down.start()

    @pl.when(has_right)
    def _():
        up.start()

    @pl.when(has_left)
    def _():
        down.wait_send()
        up.wait_recv()

    @pl.when(has_right)
    def _():
        up.wait_send()
        down.wait_recv()


def exchange(left, right):
    anywhere = pl.BlockSpec(memory_space=pl.ANY)
    return pl.pallas_call(
        functools.partial(exchange_kernel, lax.axis_size("dom")),
        in_specs=[anywhere] * 2,
        out_specs=[anywhere] * 2,
        out_shape=[jax.ShapeDtypeStruct(left.shape, left.dtype)] * 2,
        scratch_shapes=[pltpu.SemaphoreType.DMA] * 4,
        compiler_params=pltpu.CompilerParams(
            vmem_limit_bytes=4 * 1024 * 1024, collective_id=1, has_side_effects=True
        ),
        name="exchange",
    )(left, right)


def newton(gram_matrix):
    size = gram_matrix.shape[0]
    identity = (
        lax.broadcasted_iota(jnp.int32, (size, size), 0)
        == lax.broadcasted_iota(jnp.int32, (size, size), 1)
    ).astype(jnp.float32)
    frobenius = jnp.sqrt(jnp.sum(gram_matrix * gram_matrix))
    scaled = gram_matrix / frobenius
    inverse_root = None
    for repeat in range(NS_ITERS):
        if repeat == 0:
            factor = 1.5 * identity - 0.5 * scaled
            inverse_root = factor
        else:
            factor = 1.5 * identity - 0.5 * jnp.dot(
                inverse_root, scaled, precision=lax.Precision.HIGHEST
            )
            inverse_root = jnp.dot(factor, inverse_root, precision=lax.Precision.HIGHEST)
        if repeat < NS_ITERS - 1:
            scaled = jnp.dot(scaled, factor, precision=lax.Precision.HIGHEST)
    return inverse_root


def closing_kernel(domains, bands, filtered_ref, faces_ref, out_ref, shard, turned, mixing, part, weight,
                   from_dom, from_band, total,
                   send_in, recv_in, send_out, recv_out,
                   send_dom, recv_dom, send_band, recv_band, send_back, recv_back):
    dom, band = lax.axis_index("dom"), lax.axis_index("band")
    rows = part.shape[0] // domains
    state_rows = filtered_ref.shape[0]
    piece = shard.shape[1]

    def dom_peer(i):
        return (lax.rem(dom + i, domains), band)

    def band_peer(i):
        return (dom, lax.rem(band + i, bands))

    peers = [dom_peer(i) for i in range(1, domains)] + [band_peer(i) for i in range(1, bands)]
    barrier = pltpu.get_barrier_semaphore()
    for peer in peers:
        pl.semaphore_signal(barrier, inc=1, device_id=peer, device_id_type=MESH)
    pl.semaphore_wait(barrier, len(peers))

    def span(index):
        return pl.ds(pl.multiple_of(index * rows, 8), rows)

    def states_of(index):
        return pl.ds(pl.multiple_of(index * state_rows, state_rows), state_rows)

    def nodes_of(index):
        return pl.ds(pl.multiple_of(index * piece, 128), piece)

    regroup = []
    for i in range(1, bands):
        peer = band_peer(i)
        regroup.append(pltpu.make_async_remote_copy(
            src_ref=filtered_ref.at[:, nodes_of(peer[1])], dst_ref=shard.at[states_of(band)],
            send_sem=send_in.at[i], recv_sem=recv_in.at[i],
            device_id=peer, device_id_type=MESH))
    for copy in regroup:
        copy.start()
    shard[states_of(band), :] = filtered_ref[:, nodes_of(band)]
    part[...] = jnp.zeros_like(part)
    has_left = jnp.where(dom > 0, 1.0, 0.0)
    has_right = jnp.where(dom < domains - 1, 1.0, 0.0)

    def weigh(i, carry):
        shape = (128, faces_ref.shape[1])
        nodes = band * piece + i * 128 + lax.broadcasted_iota(jnp.int32, shape, 0)
        uses = jnp.where(faces_ref[0:1, :] == nodes, has_left, 0.0)
        uses = uses + jnp.where(faces_ref[1:2, :] == nodes, has_right, 0.0)
        column = 1.0 / (1.0 + jnp.sum(uses, axis=1, keepdims=True))
        row = jnp.broadcast_to(column, (128, 128)).T[:8]
        weight[:, pl.ds(pl.multiple_of(i * 128, 128), 128)] = row
        return carry

    lax.fori_loop(0, piece // 128, weigh, 0)
    for copy in regroup:
        copy.wait()

    def add_gram(i, carry):
        columns = pl.ds(pl.multiple_of(i * PIECE, PIECE), PIECE)
        value = shard[:, columns]
        part[...] += lax.dot_general(
            value * weight[0:1, columns].astype(jnp.bfloat16), value, (((1,), (1,)), ((), ())),
            preferred_element_type=jnp.float32)
        return carry

    lax.fori_loop(0, piece // PIECE, add_gram, 0)

    scatter = []
    for i in range(1, domains):
        peer = dom_peer(i)
        scatter.append(pltpu.make_async_remote_copy(
            src_ref=part.at[span(peer[0])], dst_ref=from_dom.at[i],
            send_sem=send_dom.at[i], recv_sem=recv_dom.at[i],
            device_id=peer, device_id_type=MESH))
    for copy in scatter:
        copy.start()
    own = part[span(dom), :]
    for copy in scatter:
        copy.wait()
    for i in range(1, domains):
        own = own + from_dom[i]
    from_band[band] = own
    across = []
    for i in range(1, bands):
        across.append(pltpu.make_async_remote_copy(
            src_ref=from_band.at[band], dst_ref=from_band.at[band],
            send_sem=send_band.at[i], recv_sem=recv_band.at[i],
            device_id=band_peer(i), device_id_type=MESH))
    for copy in across:
        copy.start()
    for copy in across:
        copy.wait()
    summed = from_band[0]
    for i in range(1, bands):
        summed = summed + from_band[i]
    total[span(dom), :] = summed
    back = []
    for i in range(1, domains):
        back.append(pltpu.make_async_remote_copy(
            src_ref=total.at[span(dom)], dst_ref=total.at[span(dom)],
            send_sem=send_back.at[i], recv_sem=recv_back.at[i],
            device_id=dom_peer(i), device_id_type=MESH))
    for copy in back:
        copy.start()
    for copy in back:
        copy.wait()
    mixing[...] = newton(total[...]).T.astype(jnp.bfloat16)

    def rotate(i, carry):
        columns = pl.ds(pl.multiple_of(i * PIECE, PIECE), PIECE)
        turned[:, columns] = jnp.dot(
            mixing[...], shard[:, columns], preferred_element_type=jnp.float32
        ).astype(jnp.bfloat16)
        return carry

    lax.fori_loop(0, piece // PIECE, rotate, 0)
    give = []
    for i in range(1, bands):
        peer = band_peer(i)
        give.append(pltpu.make_async_remote_copy(
            src_ref=turned.at[states_of(peer[1])], dst_ref=out_ref.at[:, nodes_of(band)],
            send_sem=send_out.at[i], recv_sem=recv_out.at[i],
            device_id=peer, device_id_type=MESH))
    for copy in give:
        copy.start()
    out_ref[:, nodes_of(band)] = turned[states_of(band), :]
    for copy in give:
        copy.wait()


PIECE = 512


def closing(filtered, faces):
    domains, bands = lax.axis_size("dom"), lax.axis_size("band")
    state_rows, nodes = filtered.shape
    size = bands * state_rows
    piece = nodes // bands
    rows = size // domains
    return pl.pallas_call(
        functools.partial(closing_kernel, domains, bands),
        in_specs=[vmem()] * 2,
        out_specs=vmem(),
        out_shape=jax.ShapeDtypeStruct(filtered.shape, jnp.bfloat16),
        scratch_shapes=[
            pltpu.VMEM((size, piece), jnp.bfloat16),
            pltpu.VMEM((size, piece), jnp.bfloat16),
            pltpu.VMEM((size, size), jnp.bfloat16),
            pltpu.VMEM((size, size), jnp.float32),
            pltpu.VMEM((8, piece), jnp.float32),
            pltpu.VMEM((domains, rows, size), jnp.float32),
            pltpu.VMEM((bands, rows, size), jnp.float32),
            pltpu.VMEM((size, size), jnp.float32),
        ] + [pltpu.SemaphoreType.DMA((bands,))] * 4
        + [pltpu.SemaphoreType.DMA((domains,))] * 2
        + [pltpu.SemaphoreType.DMA((bands,))] * 2
        + [pltpu.SemaphoreType.DMA((domains,))] * 2,
        compiler_params=pltpu.CompilerParams(
            vmem_limit_bytes=24 * 1024 * 1024, collective_id=0, has_side_effects=True
        ),
        name="closing",
    )(filtered, faces)


def body(states, cell_kinetic, cell_scale, cell_potential, connectivity, shared_nodes, cell_counts):
    domain = lax.axis_index("dom")
    domains = lax.axis_size("dom")
    state_rows, node_total = states.shape
    cells, width = connectivity.shape
    faces = shared_nodes[0]
    shared = faces.shape[1]
    tail = width // 4
    half = node_total // 2
    lanes = 2 * state_rows
    sides = jnp.stack([domain > 0, domain < domains - 1]).astype(jnp.int32)

    field_shape = jax.ShapeDtypeStruct((half, lanes), jnp.bfloat16)
    outs = [
        jax.ShapeDtypeStruct((half, lanes), jnp.float32),
        jax.ShapeDtypeStruct((shared // 2, lanes), jnp.bfloat16),
        jax.ShapeDtypeStruct((shared // 2, lanes), jnp.bfloat16),
        jax.ShapeDtypeStruct((shared, lanes), jnp.float32),
        field_shape,
    ]
    total_scratch = [
        pltpu.VMEM((node_total, state_rows), jnp.float32),
        pltpu.VMEM((2 * shared, state_rows), jnp.float32),
    ]
    scratch = [
        pltpu.VMEM((half + tail, lanes), jnp.bfloat16),
        pltpu.VMEM((half + tail, lanes), jnp.float32),
    ] + total_scratch
    group = GROUP // 2
    steps = cells // GROUP
    ops_spec = pl.BlockSpec((group, 2 * width, width), lambda g: (g, 0, 0))
    blocks = cells // 2 // GROUP
    ops, diag, local, left, right, own, previous = pl.pallas_call(
        operators_kernel,
        grid=(cells // GROUP,),
        in_specs=[smem()] * 3 + [vmem()] * 4,
        out_specs=[
            pl.BlockSpec((GROUP, width, width), lambda g: (g % blocks, g // blocks, 0)),
        ] + [vmem()] * 6,
        out_shape=[
            jax.ShapeDtypeStruct((cells // 2, 2 * width, width), jnp.bfloat16),
            jax.ShapeDtypeStruct((half, lanes), jnp.float32),
        ] + outs,
        scratch_shapes=[pltpu.VMEM((node_total + tail, 1), jnp.float32)] + scratch,
        compiler_params=params(32),
        name="operators_and_first_apply",
    )(cell_counts, cell_scale, faces, connectivity, cell_potential, cell_kinetic, states)
    current = previous
    for k in range(1, CHEB):
        halo = exchange(left, right)
        local, left, right, own, field = pl.pallas_call(
            functools.partial(next_kernel, k > 1),
            grid=(steps,),
            in_specs=[smem()] * 4 + [ops_spec] + [vmem()] * 6,
            out_specs=[vmem()] * 5,
            out_shape=outs,
            scratch_shapes=scratch,
            compiler_params=params(22),
            name="apply_next",
        )(cell_counts, cell_scale, faces, sides, ops, diag, previous, local, own, *halo)
        previous = current
        current = field
    halo = exchange(left, right)
    filtered = pl.pallas_call(
        last_kernel,
        in_specs=[smem()] * 2 + [vmem()] * 5,
        out_specs=vmem(),
        out_shape=jax.ShapeDtypeStruct((state_rows, node_total), jnp.bfloat16),
        scratch_shapes=total_scratch,
        compiler_params=params(24),
        name="finish",
    )(faces, sides, previous, local, own, *halo)
    return closing(filtered, faces)


def solution(mesh):
    in_specs = (
        P("band", "dom"),
        P(),
        P("dom"),
        P("dom", None),
        P("dom", None),
        P("dom", None, None),
        P("dom"),
    )
    out_specs = P("band", "dom")
    return jax.shard_map(body, mesh=mesh, in_specs=in_specs, out_specs=out_specs, check_vma=False)
```

```python
import functools

import jax
import jax.numpy as jnp
from jax import lax
from jax.experimental import pallas as pl
from jax.experimental.pallas import tpu as pltpu
from jax.sharding import PartitionSpec as P

CHEB = 4
NS_ITERS = 5
GROUP = 4
MESH = pl.DeviceIdType.MESH


def params(mib=56):
    return pltpu.CompilerParams(vmem_limit_bytes=mib * 1024 * 1024)


def vmem():
    return pl.BlockSpec(memory_space=pltpu.VMEM)


def smem():
    return pl.BlockSpec(memory_space=pltpu.SMEM)


def operators_kernel(counts_ref, scale_ref, faces_ref, conn_ref, pot_ref, kinetic_ref, states_ref,
                     ops_ref, diag_ref, local_ref, left_ref, right_ref, own_ref, field_ref,
                     column_sum, field, ext, total, halo):
    group, width, _ = ops_ref.shape
    step = 3 * width // 4
    half, lanes = local_ref.shape
    node_total = 2 * half
    first = pl.program_id(0) * group
    pairs = pl.num_programs(0) * group // 2

    @pl.when(pl.program_id(0) == 0)
    def _():
        column_sum[...] = jnp.zeros_like(column_sum)

        def load(i, carry):
            low = pl.ds(pl.multiple_of(i * 128, 128), 128)
            high = pl.ds(pl.multiple_of(half + i * 128, 128), 128)
            pair = jnp.concatenate([states_ref[:, low], states_ref[:, high]], axis=0)
            rounded = pair.astype(jnp.float32).T.astype(jnp.bfloat16)
            field[low, :] = rounded
            field_ref[low, :] = rounded
            ext[low, :] = jnp.zeros((128, lanes), jnp.float32)
            return carry

        lax.fori_loop(0, half // 128, load, 0, unroll=6)
        start_tail(field, ext, half)

    low_lane = lax.broadcasted_iota(jnp.int32, (1, lanes), 1) < lanes // 2
    for j in range(group):
        cell = first + j
        slots = conn_ref[pl.ds(cell, 1), :] - cell * step
        slots = jnp.where(slots < 0, slots + node_total, slots)
        hit = lax.broadcasted_iota(jnp.int32, (width, width), 0) == slots
        perm = jnp.where(hit, 1.0, 0.0).astype(jnp.bfloat16)
        rows = jnp.dot(perm, kinetic_ref[...], preferred_element_type=jnp.float32)
        operator = lax.dot_general(
            rows.astype(jnp.bfloat16), perm, (((1,), (1,)), ((), ())),
            preferred_element_type=jnp.float32,
        ).astype(jnp.bfloat16)
        ops_ref[j] = operator
        alive = jnp.where(cell < counts_ref[0], 1.0, 0.0)
        column = jnp.sum(
            jnp.where(hit, pot_ref[pl.ds(cell, 1), :] * alive, 0.0), axis=1, keepdims=True
        )
        span = pl.ds(pl.multiple_of(cell * step, 128), width)
        column_sum[span, :] = column_sum[span, :] + column
        upper = cell >= pairs
        scale = alive * scale_ref[cell]
        spread = jnp.where(
            low_lane, jnp.where(upper, 0.0, scale), jnp.where(upper, scale, 0.0)
        )
        place = jnp.where(upper, cell - pairs, cell)
        packed = pl.ds(pl.multiple_of(place * step, 128), width)
        product = jnp.dot(operator, field[packed, :], preferred_element_type=jnp.float32)
        ext[packed, :] = ext[packed, :] + product * spread

    @pl.when(pl.program_id(0) == pl.num_programs(0) - 1)
    def _():
        tail = width - step
        column_sum[:tail] = column_sum[:tail] + column_sum[node_total:]

        def weigh(base):
            rows = pl.ds(base, ROWS)
            value = jnp.where(low_lane, column_sum[rows, :], column_sum[pl.ds(half + base, ROWS), :])
            diag_ref[rows, :] = value
            ext[rows, :] = ext[rows, :] + value * field[rows, :].astype(jnp.float32)

        by_rows(half, weigh)
        finish_cells(faces_ref, local_ref, left_ref, right_ref, own_ref, ext, total, halo)


CHUNK = 64


ROWS = 768


def by_rows(total, visit):
    def step(i, carry):
        visit(pl.multiple_of(i * ROWS, ROWS))
        return carry

    lax.fori_loop(0, total // ROWS, step, 0)


def swap_halves(value):
    lanes = value.shape[1]
    return jnp.concatenate([value[:, lanes // 2 :], value[:, : lanes // 2]], axis=1)


def add_faces(sides_ref, faces_ref, own_ref, from_refs, halo, total):
    shared = faces_ref.shape[1]
    for side, packed in enumerate(from_refs):
        half, lanes = packed.shape
        base = side * shared
        rows = jnp.where(sides_ref[side] > 0, packed[...].astype(jnp.float32), 0.0)
        rows = rows + own_ref[side * half : (side + 1) * half]
        halo[base : base + half] = rows[:, : lanes // 2]
        halo[base + half : base + shared] = rows[:, lanes // 2 :]
    for side in range(2):

        def visit(i, carry, side=side):
            base = i * CHUNK
            block = halo.at[pl.ds(pl.multiple_of(side * shared + base, CHUNK), CHUNK)]
            for j in range(CHUNK):
                total[pl.ds(faces_ref[side, base + j], 1), :] = block[j : j + 1, :]
            return carry

        lax.fori_loop(0, shared // CHUNK, visit, 0)


def pick_faces(faces_ref, total, halo, own_ref, to_refs):
    shared = faces_ref.shape[1]
    half = shared // 2
    for side in range(2):

        def visit(i, carry, side=side):
            base = i * CHUNK
            block = halo.at[pl.ds(pl.multiple_of(side * shared + base, CHUNK), CHUNK)]
            for j in range(CHUNK):
                block[j : j + 1, :] = total[pl.ds(faces_ref[side, base + j], 1), :]
            return carry

        lax.fori_loop(0, shared // CHUNK, visit, 0)
        base = side * shared
        rows = jnp.concatenate([halo[base : base + half], halo[base + half : base + shared]], axis=1)
        own_ref[side * half : (side + 1) * half] = rows
        to_refs[side][...] = rows.astype(to_refs[side].dtype)


def apply_cells(counts_ref, scale_ref, ops_ref, field, ext):
    group, _, width = ops_ref.shape
    step = 3 * width // 4
    lanes = ext.shape[1]
    low = lax.broadcasted_iota(jnp.int32, (1, lanes), 1) < lanes // 2
    for j in range(group):
        cell = pl.program_id(0) * group + j
        upper = cell + pl.num_programs(0) * group
        span = pl.ds(pl.multiple_of(cell * step, 128), width)
        scale = jnp.where(cell < counts_ref[0], scale_ref[cell], 0.0)
        upper_scale = jnp.where(upper < counts_ref[0], scale_ref[upper], 0.0)
        window = field[span, :]
        both = jnp.dot(ops_ref[j], window, preferred_element_type=jnp.float32)
        ext[span, :] = ext[span, :] + jnp.where(
            low, both[:width] * scale, both[width:] * upper_scale
        )


def finish_cells(faces_ref, local_ref, left_ref, right_ref, own_ref, ext, total, halo):
    half, lanes = local_ref.shape
    tail = ext.shape[0] - half
    ext[:tail] = ext[:tail] + swap_halves(ext[half:])

    def emit(base):
        value = ext[pl.ds(base, ROWS), :]
        local_ref[pl.ds(base, ROWS), :] = value
        total[pl.ds(base, ROWS), :] = value[:, : lanes // 2]
        total[pl.ds(half + base, ROWS), :] = value[:, lanes // 2 :]

    by_rows(half, emit)
    pick_faces(faces_ref, total, halo, own_ref, (left_ref, right_ref))


def start_tail(field, ext, half):
    tail = ext.shape[0] - half
    field[half:] = swap_halves(field[:tail])
    ext[half:] = jnp.zeros((tail, ext.shape[1]), jnp.float32)


def unpack_local(old_ref, total):
    half, lanes = old_ref.shape

    def load(base):
        value = old_ref[pl.ds(base, ROWS), :]
        total[pl.ds(base, ROWS), :] = value[:, : lanes // 2]
        total[pl.ds(half + base, ROWS), :] = value[:, lanes // 2 :]

    by_rows(half, load)


def next_kernel(twice, counts_ref, scale_ref, faces_ref, sides_ref, ops_ref,
                diag_ref, prev_ref, old_ref, old_own, from_left, from_right,
                local_ref, left_ref, right_ref, own_ref, field_ref, field, ext, total, halo):
    half = local_ref.shape[0]

    @pl.when(pl.program_id(0) == 0)
    def _():
        unpack_local(old_ref, total)
        add_faces(sides_ref, faces_ref, old_own, (from_left, from_right), halo, total)

        def combine(base):
            rows = pl.ds(base, ROWS)
            value = jnp.concatenate([total[rows, :], total[pl.ds(half + base, ROWS), :]], axis=1)
            if twice:
                value = 2.0 * value - prev_ref[rows, :].astype(jnp.float32)
            value = value.astype(jnp.bfloat16)
            field[rows, :] = value
            field_ref[rows, :] = value
            ext[rows, :] = value.astype(jnp.float32) * diag_ref[rows, :]

        by_rows(half, combine)
        start_tail(field, ext, half)

    apply_cells(counts_ref, scale_ref, ops_ref, field, ext)

    @pl.when(pl.program_id(0) == pl.num_programs(0) - 1)
    def _():
        finish_cells(faces_ref, local_ref, left_ref, right_ref, own_ref, ext, total, halo)


def last_kernel(faces_ref, sides_ref, prev_ref, old_ref, old_own, from_left, from_right, field_ref,
                total, halo):
    half, lanes = old_ref.shape
    unpack_local(old_ref, total)
    add_faces(sides_ref, faces_ref, old_own, (from_left, from_right), halo, total)

    def combine(i, carry):
        low = pl.ds(pl.multiple_of(i * 128, 128), 128)
        high = pl.ds(pl.multiple_of(half + i * 128, 128), 128)
        value = jnp.concatenate([total[low, :], total[high, :]], axis=1)
        value = (2.0 * value - prev_ref[low, :].astype(jnp.float32)).T
        field_ref[:, low] = value[: lanes // 2].astype(jnp.bfloat16)
        field_ref[:, high] = value[lanes // 2 :].astype(jnp.bfloat16)
        return carry

    lax.fori_loop(0, half // 128, combine, 0, unroll=6)


def exchange_kernel(domains, left_ref, right_ref, from_left, from_right,
                    send_up, send_down, recv_up, recv_down):
    dom, band = lax.axis_index("dom"), lax.axis_index("band")
    barrier = pltpu.get_barrier_semaphore()
    has_left, has_right = dom > 0, dom < domains - 1

    @pl.when(has_left)
    def _():
        pl.semaphore_signal(barrier, inc=1, device_id=(dom - 1, band), device_id_type=MESH)

    @pl.when(has_right)
    def _():
        pl.semaphore_signal(barrier, inc=1, device_id=(dom + 1, band), device_id_type=MESH)

    pl.semaphore_wait(barrier, jnp.where(has_left & has_right, 2, 1))

    down = pltpu.make_async_remote_copy(
        src_ref=left_ref, dst_ref=from_right, send_sem=send_down, recv_sem=recv_down,
        device_id=(dom - 1, band), device_id_type=MESH)
    up = pltpu.make_async_remote_copy(
        src_ref=right_ref, dst_ref=from_left, send_sem=send_up, recv_sem=recv_up,
        device_id=(dom + 1, band), device_id_type=MESH)

    @pl.when(has_left)
    def _():
        down.start()

    @pl.when(has_right)
    def _():
        up.start()

    @pl.when(has_left)
    def _():
        down.wait_send()
        up.wait_recv()

    @pl.when(has_right)
    def _():
        up.wait_send()
        down.wait_recv()


def exchange(left, right):
    anywhere = pl.BlockSpec(memory_space=pl.ANY)
    return pl.pallas_call(
        functools.partial(exchange_kernel, lax.axis_size("dom")),
        in_specs=[anywhere] * 2,
        out_specs=[anywhere] * 2,
        out_shape=[jax.ShapeDtypeStruct(left.shape, left.dtype)] * 2,
        scratch_shapes=[pltpu.SemaphoreType.DMA] * 4,
        compiler_params=pltpu.CompilerParams(
            vmem_limit_bytes=4 * 1024 * 1024, collective_id=1, has_side_effects=True
        ),
        name="exchange",
    )(left, right)


def newton(gram_matrix):
    size = gram_matrix.shape[0]
    identity = (
        lax.broadcasted_iota(jnp.int32, (size, size), 0)
        == lax.broadcasted_iota(jnp.int32, (size, size), 1)
    ).astype(jnp.float32)
    frobenius = jnp.sqrt(jnp.sum(gram_matrix * gram_matrix))
    scaled = gram_matrix / frobenius
    inverse_root = None
    for repeat in range(NS_ITERS):
        if repeat == 0:
            factor = 1.5 * identity - 0.5 * scaled
            inverse_root = factor
        else:
            factor = 1.5 * identity - 0.5 * jnp.dot(
                inverse_root, scaled, precision=lax.Precision.HIGHEST
            )
            inverse_root = jnp.dot(factor, inverse_root, precision=lax.Precision.HIGHEST)
        if repeat < NS_ITERS - 1:
            scaled = jnp.dot(scaled, factor, precision=lax.Precision.HIGHEST)
    return inverse_root


def closing_kernel(domains, bands, filtered_ref, faces_ref, out_ref, shard, turned, mixing, part, weight,
                   from_dom, from_band, total,
                   send_in, recv_in, send_out, recv_out,
                   send_dom, recv_dom, send_band, recv_band, send_back, recv_back):
    dom, band = lax.axis_index("dom"), lax.axis_index("band")
    rows = part.shape[0] // domains
    state_rows = filtered_ref.shape[0]
    piece = shard.shape[1]

    def dom_peer(i):
        return (lax.rem(dom + i, domains), band)

    def band_peer(i):
        return (dom, lax.rem(band + i, bands))

    peers = [dom_peer(i) for i in range(1, domains)] + [band_peer(i) for i in range(1, bands)]
    barrier = pltpu.get_barrier_semaphore()
    for peer in peers:
        pl.semaphore_signal(barrier, inc=1, device_id=peer, device_id_type=MESH)
    pl.semaphore_wait(barrier, len(peers))

    def span(index):
        return pl.ds(pl.multiple_of(index * rows, 8), rows)

    def states_of(index):
        return pl.ds(pl.multiple_of(index * state_rows, state_rows), state_rows)

    def nodes_of(index):
        return pl.ds(pl.multiple_of(index * piece, 128), piece)

    regroup = []
    for i in range(1, bands):
        peer = band_peer(i)
        regroup.append(pltpu.make_async_remote_copy(
            src_ref=filtered_ref.at[:, nodes_of(peer[1])], dst_ref=shard.at[states_of(band)],
            send_sem=send_in.at[i], recv_sem=recv_in.at[i],
            device_id=peer, device_id_type=MESH))
    for copy in regroup:
        copy.start()
    shard[states_of(band), :] = filtered_ref[:, nodes_of(band)]
    part[...] = jnp.zeros_like(part)
    has_left = jnp.where(dom > 0, 1.0, 0.0)
    has_right = jnp.where(dom < domains - 1, 1.0, 0.0)

    def weigh(i, carry):
        shape = (128, faces_ref.shape[1])
        nodes = band * piece + i * 128 + lax.broadcasted_iota(jnp.int32, shape, 0)
        uses = jnp.where(faces_ref[0:1, :] == nodes, has_left, 0.0)
        uses = uses + jnp.where(faces_ref[1:2, :] == nodes, has_right, 0.0)
        column = 1.0 / (1.0 + jnp.sum(uses, axis=1, keepdims=True))
        row = jnp.broadcast_to(column, (128, 128)).T[:8]
        weight[:, pl.ds(pl.multiple_of(i * 128, 128), 128)] = row
        return carry

    lax.fori_loop(0, piece // 128, weigh, 0)
    for copy in regroup:
        copy.wait()

    def add_gram(i, carry):
        columns = pl.ds(pl.multiple_of(i * PIECE, PIECE), PIECE)
        value = shard[:, columns]
        part[...] += lax.dot_general(
            value * weight[0:1, columns].astype(jnp.bfloat16), value, (((1,), (1,)), ((), ())),
            preferred_element_type=jnp.float32)
        return carry

    lax.fori_loop(0, piece // PIECE, add_gram, 0)

    scatter = []
    for i in range(1, domains):
        peer = dom_peer(i)
        scatter.append(pltpu.make_async_remote_copy(
            src_ref=part.at[span(peer[0])], dst_ref=from_dom.at[i],
            send_sem=send_dom.at[i], recv_sem=recv_dom.at[i],
            device_id=peer, device_id_type=MESH))
    for copy in scatter:
        copy.start()
    own = part[span(dom), :]
    for copy in scatter:
        copy.wait()
    for i in range(1, domains):
        own = own + from_dom[i]
    from_band[band] = own
    across = []
    for i in range(1, bands):
        across.append(pltpu.make_async_remote_copy(
            src_ref=from_band.at[band], dst_ref=from_band.at[band],
            send_sem=send_band.at[i], recv_sem=recv_band.at[i],
            device_id=band_peer(i), device_id_type=MESH))
    for copy in across:
        copy.start()
    for copy in across:
        copy.wait()
    summed = from_band[0]
    for i in range(1, bands):
        summed = summed + from_band[i]
    total[span(dom), :] = summed
    back = []
    for i in range(1, domains):
        back.append(pltpu.make_async_remote_copy(
            src_ref=total.at[span(dom)], dst_ref=total.at[span(dom)],
            send_sem=send_back.at[i], recv_sem=recv_back.at[i],
            device_id=dom_peer(i), device_id_type=MESH))
    for copy in back:
        copy.start()
    for copy in back:
        copy.wait()
    mixing[...] = newton(total[...]).T.astype(jnp.bfloat16)

    def rotate(i, carry):
        columns = pl.ds(pl.multiple_of(i * PIECE, PIECE), PIECE)
        turned[:, columns] = jnp.dot(
            mixing[...], shard[:, columns], preferred_element_type=jnp.float32
        ).astype(jnp.bfloat16)
        return carry

    lax.fori_loop(0, piece // PIECE, rotate, 0)
    give = []
    for i in range(1, bands):
        peer = band_peer(i)
        give.append(pltpu.make_async_remote_copy(
            src_ref=turned.at[states_of(peer[1])], dst_ref=out_ref.at[:, nodes_of(band)],
            send_sem=send_out.at[i], recv_sem=recv_out.at[i],
            device_id=peer, device_id_type=MESH))
    for copy in give:
        copy.start()
    out_ref[:, nodes_of(band)] = turned[states_of(band), :]
    for copy in give:
        copy.wait()


PIECE = 512


def closing(filtered, faces):
    domains, bands = lax.axis_size("dom"), lax.axis_size("band")
    state_rows, nodes = filtered.shape
    size = bands * state_rows
    piece = nodes // bands
    rows = size // domains
    return pl.pallas_call(
        functools.partial(closing_kernel, domains, bands),
        in_specs=[vmem()] * 2,
        out_specs=vmem(),
        out_shape=jax.ShapeDtypeStruct(filtered.shape, jnp.bfloat16),
        scratch_shapes=[
            pltpu.VMEM((size, piece), jnp.bfloat16),
            pltpu.VMEM((size, piece), jnp.bfloat16),
            pltpu.VMEM((size, size), jnp.bfloat16),
            pltpu.VMEM((size, size), jnp.float32),
            pltpu.VMEM((8, piece), jnp.float32),
            pltpu.VMEM((domains, rows, size), jnp.float32),
            pltpu.VMEM((bands, rows, size), jnp.float32),
            pltpu.VMEM((size, size), jnp.float32),
        ] + [pltpu.SemaphoreType.DMA((bands,))] * 4
        + [pltpu.SemaphoreType.DMA((domains,))] * 2
        + [pltpu.SemaphoreType.DMA((bands,))] * 2
        + [pltpu.SemaphoreType.DMA((domains,))] * 2,
        compiler_params=pltpu.CompilerParams(
            vmem_limit_bytes=24 * 1024 * 1024, collective_id=0, has_side_effects=True
        ),
        name="closing",
    )(filtered, faces)


def body(states, cell_kinetic, cell_scale, cell_potential, connectivity, shared_nodes, cell_counts):
    domain = lax.axis_index("dom")
    domains = lax.axis_size("dom")
    state_rows, node_total = states.shape
    cells, width = connectivity.shape
    faces = shared_nodes[0]
    shared = faces.shape[1]
    tail = width // 4
    half = node_total // 2
    lanes = 2 * state_rows
    sides = jnp.stack([domain > 0, domain < domains - 1]).astype(jnp.int32)

    field_shape = jax.ShapeDtypeStruct((half, lanes), jnp.bfloat16)
    outs = [
        jax.ShapeDtypeStruct((half, lanes), jnp.float32),
        jax.ShapeDtypeStruct((shared // 2, lanes), jnp.bfloat16),
        jax.ShapeDtypeStruct((shared // 2, lanes), jnp.bfloat16),
        jax.ShapeDtypeStruct((shared, lanes), jnp.float32),
        field_shape,
    ]
    total_scratch = [
        pltpu.VMEM((node_total, state_rows), jnp.float32),
        pltpu.VMEM((2 * shared, state_rows), jnp.float32),
    ]
    scratch = [
        pltpu.VMEM((half + tail, lanes), jnp.bfloat16),
        pltpu.VMEM((half + tail, lanes), jnp.float32),
    ] + total_scratch
    group = GROUP
    steps = cells // (2 * GROUP)
    ops_spec = pl.BlockSpec((group, 2 * width, width), lambda g: (g, 0, 0))
    blocks = cells // 2 // GROUP
    ops, diag, local, left, right, own, previous = pl.pallas_call(
        operators_kernel,
        grid=(cells // GROUP,),
        in_specs=[smem()] * 3 + [vmem()] * 4,
        out_specs=[
            pl.BlockSpec((GROUP, width, width), lambda g: (g % blocks, g // blocks, 0)),
        ] + [vmem()] * 6,
        out_shape=[
            jax.ShapeDtypeStruct((cells // 2, 2 * width, width), jnp.bfloat16),
            jax.ShapeDtypeStruct((half, lanes), jnp.float32),
        ] + outs,
        scratch_shapes=[pltpu.VMEM((node_total + tail, 1), jnp.float32)] + scratch,
        compiler_params=params(32),
        name="operators_and_first_apply",
    )(cell_counts, cell_scale, faces, connectivity, cell_potential, cell_kinetic, states)
    current = previous
    for k in range(1, CHEB):
        halo = exchange(left, right)
        local, left, right, own, field = pl.pallas_call(
            functools.partial(next_kernel, k > 1),
            grid=(steps,),
            in_specs=[smem()] * 4 + [ops_spec] + [vmem()] * 6,
            out_specs=[vmem()] * 5,
            out_shape=outs,
            scratch_shapes=scratch,
            compiler_params=params(27),
            name="apply_next",
        )(cell_counts, cell_scale, faces, sides, ops, diag, previous, local, own, *halo)
        previous = current
        current = field
    halo = exchange(left, right)
    filtered = pl.pallas_call(
        last_kernel,
        in_specs=[smem()] * 2 + [vmem()] * 5,
        out_specs=vmem(),
        out_shape=jax.ShapeDtypeStruct((state_rows, node_total), jnp.bfloat16),
        scratch_shapes=total_scratch,
        compiler_params=params(24),
        name="finish",
    )(faces, sides, previous, local, own, *halo)
    return closing(filtered, faces)


def solution(mesh):
    in_specs = (
        P("band", "dom"),
        P(),
        P("dom"),
        P("dom", None),
        P("dom", None),
        P("dom", None, None),
        P("dom"),
    )
    out_specs = P("band", "dom")
    return jax.shard_map(body, mesh=mesh, in_specs=in_specs, out_specs=out_specs, check_vma=False)
```
